512 devices in a mesh: tm: 16 (over z_lo, core), patch: 32 (over x, y, z_hi).
Axes of the slice: x: 4, y: 4, z: 16 (z_hi: 2, z_lo: 8; z = z_hi * 8 + z_lo), core: 2. Of those that a mesh axis runs over, the one named last changes fastest.
Arguments:
- stream: bfloat16 [16, 1792, 1152], P('tm', 'patch'), may hold values from -6 to 6
- stale_keys: bfloat16 [16, 1792, 1152], P(None, 'patch', 'tm'), may hold values from -10 to 10
- stale_values: bfloat16 [16, 1792, 1152], P(None, 'patch', 'tm'), may hold values from -6 to 6
- modulation: float32 [2, 3, 1152], replicated, may hold values from -4 to 4
- w_qkv: bfloat16 [2, 3, 1152, 1152], P(None, None, 'tm'), may hold values from -0.1875 to 0.1875
- w_out: bfloat16 [2, 1152, 1152], P(None, 'tm'), may hold values from -0.1875 to 0.1875
- qk_gain: float32 [2, 2, 72], replicated, may hold values from 1.4 to 7
Outputs:
- output: bfloat16 [16, 1792, 1152], P('tm', 'patch')
The draws below stay inside these ranges and needn't reach their ends.
All inputs are finite; a program needn't handle non-finite values.
Results may differ from the reference program's by a relative error of at most 0.035.
Values may be sent and summed in bfloat16 or wider, within the bound.
No kernel may reach another device: no remote copies, remote signals or barrier semaphores. Data moves between devices by JAX's collectives and lax.ppermute only.
A program may use at most 64 MiB of HBM per device.

```python
import jax
import jax.numpy as jnp
from jax import lax

D = 1152
HEADS = 16
HEAD_DIM = 72
TOK_FRAME_DEV = 56
FRAMES = 16
SPATIAL = 1792
N_TM = 16


def draw_qk_gain(key, part):
    key = jax.random.fold_in(key, 7)
    unit = jax.random.uniform(key, (2, 2, HEAD_DIM), jnp.float32)
    return 1.4 + 0.8 * unit


def block_levels(own_key, extent, split, least, largest):
    loudness, own = 1.0, jax.random.fold_in(own_key, 6)
    for dim, blocks in split:
        steps = jnp.exp(jax.random.uniform(jax.random.fold_in(own, dim), (blocks,), jnp.float32, least / len(split), largest / len(split)))
        loudness = loudness * jnp.repeat(steps, extent[dim] // blocks).reshape([-1 if axis == dim else 1 for axis in range(len(extent))])
    return loudness


def noise(key, shape, scale, limit, cuts=(), held_as=jnp.bfloat16):
    level = block_levels(key, shape, cuts, -0.22, 0.18) if cuts else 1.0
    array = jax.random.normal(key, shape, jnp.float32) * scale * level
    return jnp.minimum(jnp.maximum(array, -limit), limit).astype(held_as)


def setup_inputs(seed: int = 0) -> dict:
    streams_of = jax.random.split(jax.random.key(seed), 8)
    stream = noise(streams_of[0], (FRAMES, SPATIAL, D), 1.0, 6.0, ((0, 16), (1, 32)))
    stale_keys = noise(streams_of[1], (FRAMES, SPATIAL, D), 1.8, 10.0, ((1, 32), (2, 16)))
    stale_values = noise(streams_of[2], (FRAMES, SPATIAL, D), 1.0, 6.0, ((1, 32), (2, 16)))
    modulation = noise(streams_of[3], (2, 3, D), 0.7, 4.0, (), jnp.float32)
    w_qkv = noise(streams_of[4], (2, 3, D, D), D ** -0.5, 0.1875, ((2, 16),))
    w_out = noise(streams_of[5], (2, D, D), D ** -0.5, 0.1875, ((1, 16),))
    qk_gain = draw_qk_gain(jax.random.fold_in(streams_of[7], 71), 0)
    return {"stream": stream, "stale_keys": stale_keys, "stale_values": stale_values, "modulation": modulation, "w_qkv": w_qkv, "w_out": w_out, "qk_gain": qk_gain}


EPS = 1e-06

def softmax_rows(scores):
    top = lax.optimization_barrier(jnp.max(scores, axis=-1, keepdims=True))
    expo = jnp.exp(scores - top)
    return expo / lax.optimization_barrier(jnp.sum(expo, axis=-1, keepdims=True))

def modulate(stream, shift, scale):
    values = stream.astype(jnp.float32)
    center = lax.optimization_barrier(jnp.mean(values, axis=-1, keepdims=True))
    spread = lax.optimization_barrier(jnp.mean(jnp.square(values - center), axis=-1, keepdims=True))
    normed = (values - center) * lax.rsqrt(spread + EPS)
    return (normed * (1.0 + scale) + shift).astype(jnp.bfloat16)

def head_norm(values, gain):
    factor = lax.rsqrt(lax.optimization_barrier(jnp.mean(values * values, axis=-1, keepdims=True)) + EPS)
    return (values * factor * gain).astype(jnp.bfloat16)

def projections(stream, weights, gains, shift, scale):
    frames, spatial = (stream.shape[0], stream.shape[1])
    hmod = modulate(stream, shift, scale).reshape(frames * spatial, D)

    def one(matrix):
        raw = lax.dot_general(hmod, matrix, (((1,), (1,)), ((), ())), preferred_element_type=jnp.float32)
        return raw.reshape(frames, spatial, HEADS, HEAD_DIM)
    query = head_norm(one(weights[0]), gains[0])
    keys = head_norm(one(weights[1]), gains[1])
    values = one(weights[2]).astype(jnp.bfloat16)
    return (query, keys, values)

def spatial(query, keys, values, old_keys, old_values):
    block = jnp.arange(SPATIAL, dtype=jnp.int32) // TOK_FRAME_DEV
    same = (block[:, None] == block[None, :])[None]
    factor = HEAD_DIM ** (-0.5)

    def one(items):
        q, k, v, ok, ov = [a.astype(jnp.float32) for a in items]
        fresh = jnp.einsum('qhd,khd->hqk', q, k)
        older = jnp.einsum('qhd,khd->hqk', q, ok)
        scores = jnp.where(same, fresh, older) * factor
        weights = lax.optimization_barrier(softmax_rows(scores).astype(jnp.bfloat16)).astype(jnp.float32)
        near = jnp.einsum('hqk,khd->qhd', jnp.where(same, weights, jnp.float32(0.0)), v)
        far = jnp.einsum('hqk,khd->qhd', jnp.where(same, jnp.float32(0.0), weights), ov)
        return (near + far).astype(jnp.bfloat16)
    return lax.map(one, (query, keys, values, old_keys, old_values))

def temporal(query, keys, values):
    factor = HEAD_DIM ** (-0.5)
    scores = jnp.einsum('fshd,gshd->shfg', query.astype(jnp.float32), keys.astype(jnp.float32)) * factor
    weights = lax.optimization_barrier(softmax_rows(scores).astype(jnp.bfloat16)).astype(jnp.float32)
    return jnp.einsum('shfg,gshd->fshd', weights, values.astype(jnp.float32)).astype(jnp.bfloat16)

def out_sum(attn, matrix):
    width = D // N_TM

    def add(total, group):
        start = (group * width).astype(jnp.int32)
        piece = lax.dynamic_slice_in_dim(attn, start, width, 1)
        rows = lax.dynamic_slice_in_dim(matrix, start, width, 0)
        part = jnp.dot(piece, rows, preferred_element_type=jnp.float32).astype(jnp.bfloat16)
        return (total + part.astype(jnp.float32), None)
    total, _ = lax.scan(add, jnp.zeros((attn.shape[0], D), jnp.float32), jnp.arange(N_TM, dtype=jnp.int32))
    return total

def reference(stream, stale_keys, stale_values, modulation, w_qkv, w_out, qk_gain):
    frames, spatial_len = (stream.shape[0], stream.shape[1])
    shape4 = (frames, spatial_len, HEADS, HEAD_DIM)
    query, keys, values = projections(stream, w_qkv[0], qk_gain[0], modulation[0, 0], modulation[0, 1])
    attn = spatial(query, keys, values, stale_keys.reshape(shape4), stale_values.reshape(shape4))
    proj = out_sum(attn.reshape(frames * spatial_len, D), w_out[0]).reshape(frames, spatial_len, D)
    middle = (stream.astype(jnp.float32) + modulation[0, 2] * proj).astype(jnp.bfloat16)
    query, keys, values = projections(middle, w_qkv[1], qk_gain[1], modulation[1, 0], modulation[1, 1])
    attn = temporal(query, keys, values)
    proj = out_sum(attn.reshape(frames * spatial_len, D), w_out[1]).reshape(frames, spatial_len, D)
    return (middle.astype(jnp.float32) + modulation[1, 2] * proj).astype(jnp.bfloat16)
```

```python
import functools

import jax
import jax.numpy as jnp
from jax import lax
from jax.experimental import pallas as pl
from jax.experimental.pallas import tpu as pltpu
from jax.sharding import Mesh
from jax.sharding import PartitionSpec as P

HEAD_DIM = 72
EPS = 1e-06
AXES = ("z", "c", "x", "y", "h")
SIZES = (8, 2, 4, 4, 2)
ROWS = 56
PLANE = 16
QBLOCK = 4 * ROWS
NEG = -1e30
VMEM_LIMIT = 48 * 1024 * 1024
NT = (((1,), (1,)), ((), ()))


def modulate(stream, shift, scale):
    values = stream.astype(jnp.float32)
    center = jnp.mean(values, axis=-1, keepdims=True)
    spread = jnp.mean(jnp.square(values - center), axis=-1, keepdims=True)
    normed = (values - center) * lax.rsqrt(spread + EPS)
    return (normed * (1.0 + scale) + shift).astype(jnp.bfloat16)


def head_norm(values, gain):
    factor = lax.rsqrt(jnp.mean(values * values, axis=-1, keepdims=True) + EPS)
    return (values * factor * gain).astype(jnp.bfloat16)


def dot(a, b, dims=(((1,), (0,)), ((), ()))):
    return lax.dot_general(a, b, dims, preferred_element_type=jnp.float32)


def spatial_kernel(tok, w, gain, keys, vals, wout, rowp, colp, out, q_s, k_s, v_s):
    step = pl.program_id(0)
    factor = HEAD_DIM ** (-0.5)

    @pl.when(step == 0)
    def _():
        raw = dot(tok[...], w[...], NT)
        q_s[...] = head_norm(raw[:, :HEAD_DIM], gain[0:1])
        k_s[...] = head_norm(raw[:, HEAD_DIM : 2 * HEAD_DIM], gain[1:2])
        v_s[...] = raw[:, 2 * HEAD_DIM :].astype(jnp.bfloat16)

    at = pl.ds(pl.multiple_of(step * QBLOCK, QBLOCK), QBLOCK)
    q = q_s[at]
    rows = rowp[at]
    old = dot(q, keys[...], NT)
    old = jnp.where(rows == colp[...], NEG, old)
    new = dot(q, k_s[at], NT)
    r_id = lax.broadcasted_iota(jnp.int32, (QBLOCK, QBLOCK), 0) // ROWS
    c_id = lax.broadcasted_iota(jnp.int32, (QBLOCK, QBLOCK), 1) // ROWS
    new = jnp.where(r_id == c_id, new, NEG)
    top = jnp.maximum(jnp.max(old, axis=1, keepdims=True), jnp.max(new, axis=1, keepdims=True))
    e_old = jnp.exp((old - top) * factor)
    e_new = jnp.exp((new - top) * factor)
    total = jnp.sum(e_old, axis=1, keepdims=True) + jnp.sum(e_new, axis=1, keepdims=True)
    mixed = dot(e_old.astype(jnp.bfloat16), vals[...]) + dot(e_new.astype(jnp.bfloat16), v_s[at])
    attn = (mixed / total).astype(jnp.bfloat16)
    out[...] = dot(attn, wout[...]).astype(jnp.bfloat16)


def spatial(tok, w, gain, keys, vals, wout, rowp, colp):
    rows, width = tok.shape
    whole = lambda a: pl.BlockSpec(a.shape, lambda i: (0,) * a.ndim)
    args = (tok, w, gain, keys, vals, wout, rowp, colp)
    return pl.pallas_call(
        spatial_kernel,
        grid=(rows // QBLOCK,),
        in_specs=[whole(a) for a in args],
        out_specs=pl.BlockSpec((QBLOCK, width), lambda i: (i, 0)),
        out_shape=jax.ShapeDtypeStruct((rows, width), jnp.bfloat16),
        scratch_shapes=[pltpu.VMEM((rows, HEAD_DIM), jnp.bfloat16)] * 3,
        compiler_params=pltpu.CompilerParams(vmem_limit_bytes=VMEM_LIMIT),
        cost_estimate=pl.CostEstimate(
            flops=1200_000_000, bytes_accessed=6_000_000, transcendentals=1_800_000
        ),
        name="spatial",
    )(*args)


def qkv_kernel(tok, w_own, w_sib, gain, own, sib):
    for w, out in ((w_own, own), (w_sib, sib)):
        raw = dot(tok[...], w[...], NT)
        out[0] = head_norm(raw[:, :HEAD_DIM], gain[0:1])
        out[1] = head_norm(raw[:, HEAD_DIM : 2 * HEAD_DIM], gain[1:2])
        out[2] = raw[:, 2 * HEAD_DIM :].astype(jnp.bfloat16)


def qkv_pair(tok, w_own, w_sib, gain):
    shape = jax.ShapeDtypeStruct((3, tok.shape[0], HEAD_DIM), jnp.bfloat16)
    return pl.pallas_call(
        qkv_kernel,
        out_shape=(shape, shape),
        compiler_params=pltpu.CompilerParams(vmem_limit_bytes=VMEM_LIMIT),
        cost_estimate=pl.CostEstimate(flops=450_000_000, bytes_accessed=3_000_000, transcendentals=0),
        name="qkv",
    )(tok, w_own, w_sib, gain)


def temporal_kernel(own, other, out):
    factor = HEAD_DIM ** (-0.5)
    half = own.shape[1]
    size = 2 * half * 8
    r_id = lax.broadcasted_iota(jnp.int32, (size, size), 0) % 8
    c_id = lax.broadcasted_iota(jnp.int32, (size, size), 1) % 8
    same = r_id == c_id

    for g in range(ROWS // 8):
        at = slice(8 * g, 8 * g + 8)

        def pick(i):
            return jnp.concatenate(
                [r[i, f, at].astype(jnp.float32) for r in (own, other) for f in range(half)], axis=0
            ).astype(jnp.bfloat16)

        scores = jnp.where(same, dot(pick(0), pick(1), NT), NEG)
        top = jnp.max(scores, axis=1, keepdims=True)
        expo = jnp.exp((scores - top) * factor)
        weights = (expo / jnp.sum(expo, axis=1, keepdims=True)).astype(jnp.bfloat16)
        mixed = dot(weights, pick(2)).astype(jnp.bfloat16)
        for f in range(2 * half):
            out[f // half, f % half, at] = mixed[8 * f : 8 * f + 8]


def temporal(own, other):
    shape = jax.ShapeDtypeStruct((2,) + own.shape[1:], jnp.bfloat16)
    return pl.pallas_call(
        temporal_kernel,
        out_shape=shape,
        compiler_params=pltpu.CompilerParams(vmem_limit_bytes=VMEM_LIMIT),
        cost_estimate=pl.CostEstimate(flops=50_000_000, bytes_accessed=1_000_000, transcendentals=120_000),
        name="temporal",
    )(own, other)


def flat(z, c, x, y, h):
    index = 0
    for value, size in zip((z, c, x, y, h), SIZES):
        index = index * size + value
    return index


def spread(offset):
    pairs = []
    for x in range(4):
        for y in range(4):
            q = 4 * x + y
            for h in range(2):
                start = 8 * h + q // 2
                end = (start + offset) % 16
                pairs.append(
                    (flat(start % 8, q % 2, x, y, start // 8), flat(end % 8, q % 2, x, y, end // 8))
                )
    return pairs


SWAP = [(0, 1), (1, 0)]


def column_weights(w):
    q = 4 * lax.axis_index("x") + lax.axis_index("y")
    here = 2 * lax.axis_index("z") + lax.axis_index("c")
    mine = jnp.where(q == here, w, jnp.zeros_like(w))
    for offset in (4, -3, 3, -2, 2, -1, 1):
        mine = mine + lax.ppermute(w, AXES, spread(offset))
    return mine + lax.ppermute(mine, "c", SWAP)


def local(stream, stale_keys, stale_values, modulation, w_qkv, w_out, qk_gain):
    width = stream.shape[2]
    h = lax.axis_index("h")
    c = lax.axis_index("c")

    packed = jnp.concatenate([w_qkv[0].reshape(3 * HEAD_DIM, width), w_out[0]], axis=0)
    w_col = column_weights(packed)
    w_full = lax.all_gather(w_out[1], ("z", "c"), axis=0)
    w_own = w_qkv[1].reshape(3 * HEAD_DIM, width)
    w_sib = lax.ppermute(w_own, "c", SWAP)

    main = jnp.concatenate([stale_keys, stale_values[:, :, :56]], axis=2)
    tail = stale_values[:, :, 56:].reshape(16, 7, 8, 16).transpose(0, 2, 1, 3).reshape(16, 8, 112)
    tail = jnp.pad(tail, ((0, 0), (0, 0), (0, 16)))
    chunk = jnp.concatenate([main, tail], axis=1)
    chunk = jnp.broadcast_to(chunk[:, None], (16, 2, 64, 128)).reshape(32, 64, 128)
    old = lax.all_to_all(chunk, ("z", "c", "h"), 0, 0, tiled=True)
    old = lax.all_to_all(old.reshape(16, 2, 64, 128), ("x", "y"), 0, 0, tiled=True)
    keys = old[:, :, :56, :72].reshape(-1, HEAD_DIM)
    rest = old[:, :, 56:, :112].reshape(16, 2, 8, 7, 16).transpose(0, 1, 3, 2, 4).reshape(16, 2, 56, 16)
    values = jnp.concatenate([old[:, :, :56, 72:], rest], axis=3).reshape(-1, HEAD_DIM)

    hmod = modulate(stream[0], modulation[0, 0], modulation[0, 1])
    tok = lax.all_to_all(
        jnp.broadcast_to(hmod[None], (PLANE,) + hmod.shape), ("x", "y"), 0, 0, tiled=True
    ).reshape(PLANE * ROWS, width)
    rowp = (2 * (lax.iota(jnp.int32, PLANE * ROWS) // ROWS) + h)[:, None]
    colp = (lax.iota(jnp.int32, 2 * PLANE * ROWS) // ROWS)[None, :]
    part = spatial(
        tok, w_col[: 3 * HEAD_DIM], qk_gain[0], keys, values, w_col[3 * HEAD_DIM :], rowp, colp
    )
    part = lax.all_to_all(part.reshape(PLANE, ROWS, width), ("x", "y"), 0, 0, tiled=True)
    summed = jnp.sum(part.astype(jnp.float32), axis=0)
    middle = (stream[0].astype(jnp.float32) + modulation[0, 2] * summed).astype(jnp.bfloat16)

    hmod = modulate(middle, modulation[1, 0], modulation[1, 1])
    tok = lax.all_gather(hmod, "z", axis=0).reshape(8 * ROWS, width)
    own, sib = qkv_pair(tok, w_own, w_sib, qk_gain[1])
    other = lax.ppermute(sib, "c", SWAP)
    shape = (3, 8, ROWS, HEAD_DIM)
    attn = temporal(own.reshape(shape), other.reshape(shape))
    attn = jnp.where(c == 0, attn, attn[::-1]).transpose(1, 0, 2, 3).reshape(16, ROWS, HEAD_DIM)
    attn = lax.all_to_all(attn, ("z", "c"), 0, 0, tiled=True)
    attn = attn.transpose(1, 0, 2).reshape(ROWS, width)
    summed = dot(attn, w_full.reshape(width, width))
    out = (middle.astype(jnp.float32) + modulation[1, 2] * summed).astype(jnp.bfloat16)
    return out[None]


def solution(mesh):
    wide = Mesh(mesh.devices.reshape(SIZES), AXES)
    tm, patch = ("z", "c"), ("x", "y", "h")
    placed = (
        P(tm, patch, None),
        P(None, patch, tm),
        P(None, patch, tm),
        P(),
        P(None, None, tm, None),
        P(None, tm, None),
        P(),
    )
    return jax.shard_map(
        local, mesh=wide, in_specs=placed, out_specs=P(tm, patch, None), check_vma=False
    )
```

```python
import functools

import jax
import jax.numpy as jnp
from jax import lax
from jax.experimental import pallas as pl
from jax.experimental.pallas import tpu as pltpu
from jax.sharding import Mesh
from jax.sharding import PartitionSpec as P

HEAD_DIM = 72
EPS = 1e-06
AXES = ("z", "c", "x", "y", "h")
SIZES = (8, 2, 4, 4, 2)
ROWS = 56
PLANE = 16
QBLOCK = 4 * ROWS
NEG = -1e30
VMEM_LIMIT = 48 * 1024 * 1024
NT = (((1,), (1,)), ((), ()))


def normed(values, shift, scale):
    center = jnp.mean(values, axis=-1, keepdims=True)
    spread = jnp.mean(jnp.square(values - center), axis=-1, keepdims=True)
    unit = (values - center) * lax.rsqrt(spread + EPS)
    return (unit * (1.0 + scale) + shift).astype(jnp.bfloat16)


def head_norm(values, gain):
    factor = lax.rsqrt(jnp.mean(values * values, axis=-1, keepdims=True) + EPS)
    return (values * factor * gain).astype(jnp.bfloat16)


def dot(a, b, dims=(((1,), (0,)), ((), ()))):
    return lax.dot_general(a, b, dims, preferred_element_type=jnp.float32)


def call(kernel, args, out_shape, name, scratch=(), flops=0, moved=0, trans=0, grid=None, specs=None):
    extra = {} if grid is None else {"grid": grid, "in_specs": specs[0], "out_specs": specs[1]}
    return pl.pallas_call(
        kernel,
        out_shape=out_shape,
        scratch_shapes=list(scratch),
        compiler_params=pltpu.CompilerParams(vmem_limit_bytes=VMEM_LIMIT),
        cost_estimate=pl.CostEstimate(flops=flops, bytes_accessed=moved, transcendentals=trans),
        name=name,
        **extra,
    )(*args)


def modulate_kernel(x, mod, out):
    out[...] = normed(x[...].astype(jnp.float32), mod[0:1], mod[1:2])


def modulate(x, mod):
    shape = jax.ShapeDtypeStruct(x.shape, jnp.bfloat16)
    return call(modulate_kernel, (x, mod), shape, "modulate", moved=300_000)


def qkv_kernel(*refs):
    toks, (w, gain, out) = refs[:-3], refs[-3:]
    rows = toks[0].shape[0]
    for i, tok in enumerate(toks):
        raw = dot(tok[...], w[...], NT)
        at = slice(i * rows, (i + 1) * rows)
        out[0, at] = head_norm(raw[:, :HEAD_DIM], gain[0:1])
        out[1, at] = head_norm(raw[:, HEAD_DIM : 2 * HEAD_DIM], gain[1:2])
        out[2, at] = raw[:, 2 * HEAD_DIM :].astype(jnp.bfloat16)


def qkv(toks, w, gain):
    rows = sum(t.shape[0] for t in toks)
    shape = jax.ShapeDtypeStruct((3, rows, HEAD_DIM), jnp.bfloat16)
    flops = 2 * rows * w.shape[0] * w.shape[1]
    return call(qkv_kernel, (*toks, w, gain), shape, "qkv", flops=flops, moved=3_000_000)


def spatial_kernel(order, q, old, rowp, colp, w, out, vals_s, old_s, part_s):
    step = pl.program_id(0)
    factor = HEAD_DIM ** (-0.5)

    @pl.when(step == 0)
    def _():
        raw = old[...].astype(jnp.float32)
        vals_s[:, :, :56] = raw[:, :56, HEAD_DIM:]
        for j in range(7):
            vals_s[:, 8 * j : 8 * j + 8, 56:72] = raw[:, 56:, 16 * j : 16 * j + 16]
        old_s[...] = raw[:, :56, :HEAD_DIM].reshape(old_s.shape).astype(jnp.bfloat16)

    at = pl.ds(pl.multiple_of(step * QBLOCK, QBLOCK), QBLOCK)
    query, key, value = q[0, at], q[1, at], q[2, at]
    old_values = vals_s[...].reshape(old_s.shape).astype(jnp.bfloat16)
    far = dot(query, old_s[...], NT)
    far = jnp.where(rowp[at] == colp[...], NEG, far)
    near = dot(query, key, NT)
    r_id = lax.broadcasted_iota(jnp.int32, (QBLOCK, QBLOCK), 0) // ROWS
    c_id = lax.broadcasted_iota(jnp.int32, (QBLOCK, QBLOCK), 1) // ROWS
    near = jnp.where(r_id == c_id, near, NEG)
    top = jnp.maximum(jnp.max(far, axis=1, keepdims=True), jnp.max(near, axis=1, keepdims=True))
    e_far = jnp.exp((far - top) * factor)
    e_near = jnp.exp((near - top) * factor)
    total = jnp.sum(e_far, axis=1, keepdims=True) + jnp.sum(e_near, axis=1, keepdims=True)
    mixed = dot(e_far.astype(jnp.bfloat16), old_values) + dot(e_near.astype(jnp.bfloat16), value)
    part_s[...] = dot((mixed / total).astype(jnp.bfloat16), w[...])
    for j in range(QBLOCK // ROWS):
        piece = part_s[j * ROWS : (j + 1) * ROWS].astype(jnp.bfloat16)
        out[order[step * (QBLOCK // ROWS) + j]] = piece


def spatial(order, q, old, rowp, colp, w):
    rows = q.shape[1]
    whole = lambda a: pl.BlockSpec(a.shape, lambda i: (0,) * a.ndim)
    out = jax.ShapeDtypeStruct((PLANE, ROWS, w.shape[1]), jnp.bfloat16)
    args = (q, old, rowp, colp, w)
    specs = (
        [pl.BlockSpec(memory_space=pltpu.SMEM)] + [whole(a) for a in args],
        pl.BlockSpec(out.shape, lambda i: (0, 0, 0)),
    )
    scratch = (
        pltpu.VMEM((2 * PLANE, ROWS, HEAD_DIM), jnp.float32),
        pltpu.VMEM((2 * PLANE * ROWS, HEAD_DIM), jnp.bfloat16),
        pltpu.VMEM((QBLOCK, w.shape[1]), jnp.float32),
    )
    return call(
        spatial_kernel, (order, *args), out, "spatial", scratch, flops=600_000_000, moved=2_000_000,
        trans=1_800_000, grid=(rows // QBLOCK,), specs=specs,
    )


def combine_kernel(part, resid, mod, middle, hmod):
    summed = part[0].astype(jnp.float32)
    for i in range(1, part.shape[0]):
        summed = summed + part[i].astype(jnp.float32)
    mid = (resid[...].astype(jnp.float32) + mod[0:1] * summed).astype(jnp.bfloat16)
    middle[...] = mid
    hmod[...] = normed(mid.astype(jnp.float32), mod[1:2], mod[2:3])


def combine(part, resid, mod):
    out = jax.ShapeDtypeStruct(resid.shape, jnp.bfloat16)
    return call(combine_kernel, (part, resid, mod), (out, out), "combine", moved=2_500_000)


def project_kernel(heads, attn, w, resid, gate, out, attn_s):
    for g in range(PLANE):
        attn_s[:, g * HEAD_DIM : (g + 1) * HEAD_DIM] = attn[heads[g]].astype(jnp.float32)
    summed = dot(attn_s[...].astype(jnp.bfloat16), w[...])
    out[...] = (resid[...].astype(jnp.float32) + gate[...] * summed).astype(jnp.bfloat16)


def project(heads, attn, w, resid, gate):
    out = jax.ShapeDtypeStruct(resid.shape, jnp.bfloat16)
    vmem = pl.BlockSpec(memory_space=pltpu.VMEM)
    specs = ([pl.BlockSpec(memory_space=pltpu.SMEM)] + [vmem] * 4, vmem)
    return call(
        project_kernel, (heads, attn, w, resid, gate), out, "project", (pltpu.VMEM(resid.shape, jnp.float32),),
        flops=150_000_000, moved=3_200_000, grid=(), specs=specs,
    )


def temporal_kernel(place, own, other, out):
    factor = HEAD_DIM ** (-0.5)
    half = own.shape[1]
    size = 2 * half * 8
    r_id = lax.broadcasted_iota(jnp.int32, (size, size), 0) % 8
    c_id = lax.broadcasted_iota(jnp.int32, (size, size), 1) % 8
    same = r_id == c_id

    for g in range(ROWS // 8):
        at = slice(8 * g, 8 * g + 8)

        def pick(i):
            return jnp.concatenate(
                [r[i, f, at].astype(jnp.float32) for r in (own, other) for f in range(half)], axis=0
            ).astype(jnp.bfloat16)

        scores = jnp.where(same, dot(pick(0), pick(1), NT), NEG)
        top = jnp.max(scores, axis=1, keepdims=True)
        expo = jnp.exp((scores - top) * factor)
        weights = (expo / jnp.sum(expo, axis=1, keepdims=True)).astype(jnp.bfloat16)
        mixed = dot(weights, pick(2)).astype(jnp.bfloat16)
        for f in range(2 * half):
            out[place[f], at] = mixed[8 * f : 8 * f + 8]


def temporal(place, own, other):
    shape = jax.ShapeDtypeStruct((2 * own.shape[1],) + own.shape[2:], jnp.bfloat16)
    vmem = pl.BlockSpec(memory_space=pltpu.VMEM)
    specs = ([pl.BlockSpec(memory_space=pltpu.SMEM), vmem, vmem], vmem)
    return call(
        temporal_kernel, (place, own, other), shape, "temporal", flops=50_000_000, moved=1_000_000,
        trans=120_000, grid=(), specs=specs,
    )


def flat(z, c, x, y, h):
    index = 0
    for value, size in zip((z, c, x, y, h), SIZES):
        index = index * size + value
    return index


def turn(z):
    return 2 * z + 8 * (z % 2)


def shifted():
    pairs = []
    for x in range(4):
        for y in range(4):
            q = 4 * x + y
            for ring in range(16):
                step = (((q + turn(ring % 8)) % 16) // 2 - ring % 8) % 8
                if step > 4 or (step == 4 and ring // 2 % 2):
                    step -= 8
                a, b = (ring + step) % 16, ring
                pairs.append((flat(a % 8, q % 2, x, y, a // 8), flat(b % 8, q % 2, x, y, b // 8)))
    return pairs


def rolled():
    return [
        [flat(z, c, q // 4, q % 4, h) for q in ((i - turn(z)) % PLANE for i in range(PLANE))]
        for z in range(8)
        for c in range(2)
        for h in range(2)
    ]


SWAP = [(0, 1), (1, 0)]


def plane_gather(block):
    def by(part, axis):
        return [part] + [
            lax.ppermute(part, axis, [(i, i ^ k) for i in range(4)]) for k in (1, 2, 3)
        ]

    return by(jnp.concatenate(by(block, "x"), axis=0), "y")


def line_gather(block):
    def to(part, k):
        return lax.ppermute(part, "z", [(z, z ^ k) for z in range(8)])

    far, *near = [to(block, k) for k in (4, 3, 2, 1)]
    return [block, *near[::-1], far] + [to(far, k) for k in (1, 2, 3)]


def together(steps, always, *args):
    shapes = jax.eval_shape(steps, *args)
    blank = lambda *_: jax.tree.map(lambda s: jnp.zeros(s.shape, s.dtype), shapes)
    return lax.cond(always, steps, blank, *args)


def local(stream, stale_keys, stale_values, modulation, w_qkv, w_out, qk_gain):
    width = stream.shape[2]
    x, y, z, c, h = [lax.axis_index(a) for a in ("x", "y", "z", "c", "h")]
    column = 4 * x + y
    mine = column % 2 == c
    blocks = jnp.arange(16, dtype=jnp.int32)

    main = jnp.concatenate([stale_keys, stale_values[:, :, :56]], axis=2)
    tail = stale_values[:, :, 56:].reshape(16, 7, 8, 16).transpose(0, 2, 1, 3).reshape(16, 8, 112)
    tail = jnp.pad(tail, ((0, 0), (0, 0), (0, 16)))
    chunk = jnp.concatenate([main, tail], axis=1)
    chunk = jnp.broadcast_to(chunk[:, None], (16, 2, 64, 128)).reshape(32, 64, 128)
    old = lax.all_to_all(chunk, ("z", "c", "h"), 0, 0, tiled=True)

    def gathered(first, rows):
        have = lax.ppermute(rows, AXES, shifted())
        return (*plane_gather(modulate(first, modulation[0])), have)

    rows = jnp.concatenate([w_qkv[0].reshape(3 * HEAD_DIM, width), w_out[0], w_out[1]], axis=0)
    toks = together(gathered, z >= 0, stream[0], rows)
    old, toks = lax.optimization_barrier((old, toks))
    old = lax.all_to_all(
        old.reshape(16, 2, 64, 128), AXES, 0, 0, axis_index_groups=rolled(), tiled=True
    )
    w_col = jnp.where(mine, toks[4], lax.ppermute(toks[4], "c", SWAP))
    w_last = lax.all_gather(w_col[4 * HEAD_DIM :], ("x", "y"), axis=0).reshape(width, width)
    w_own = w_qkv[1].reshape(3 * HEAD_DIM, width)
    order = 4 * (x ^ (blocks % 4)) + (y ^ (blocks // 4))
    fresh = qkv(toks[:4], w_col[: 3 * HEAD_DIM], qk_gain[0])
    rowp = jnp.repeat(2 * order + h, ROWS)[:, None]
    colp = jnp.repeat((lax.iota(jnp.int32, 2 * PLANE) - 2 * turn(z)) % (2 * PLANE), ROWS)[None, :]
    w_head = w_col[3 * HEAD_DIM : 4 * HEAD_DIM]
    part = spatial(order, fresh, old.reshape(2 * PLANE, 64, 128), rowp, colp, w_head)
    part = lax.all_to_all(part, ("x", "y"), 0, 0, tiled=True)
    middle, hmod = combine(part, stream[0], jnp.concatenate([modulation[0, 2:], modulation[1, :2]]))

    toks = [jnp.concatenate(line_gather(hmod), axis=0)]
    w_sib = lax.ppermute(w_own, "c", SWAP)
    sib = qkv(toks, w_sib, qk_gain[1])
    other = lax.ppermute(sib, "c", SWAP)
    own = qkv(toks, w_own, qk_gain[1])
    shape = (3, 8, ROWS, HEAD_DIM)
    place = 2 * (z ^ (blocks % 8)) + (c ^ (blocks // 8))
    attn = temporal(place, own.reshape(shape), other.reshape(shape))
    attn = lax.all_to_all(attn, ("z", "c"), 0, 0, tiled=True)
    out = project((blocks + turn(z)) % 16, attn, w_last, middle, modulation[1, 2:])
    return out[None]


def solution(mesh):
    wide = Mesh(mesh.devices.reshape(SIZES), AXES)
    tm, patch = ("z", "c"), ("x", "y", "h")
    placed = (
        P(tm, patch, None),
        P(None, patch, tm),
        P(None, patch, tm),
        P(),
        P(None, None, tm, None),
        P(None, tm, None),
        P(),
    )
    return jax.shard_map(
        local, mesh=wide, in_specs=placed, out_specs=P(tm, patch, None), check_vma=False
    )
```

```python
import functools

import jax
import jax.numpy as jnp
from jax import lax
from jax.experimental import pallas as pl
from jax.experimental.pallas import tpu as pltpu
from jax.sharding import Mesh
from jax.sharding import PartitionSpec as P

HEAD_DIM = 72
EPS = 1e-06
AXES = ("z", "c", "x", "y", "h")
SIZES = (8, 2, 4, 4, 2)
ROWS = 56
PLANE = 16
QBLOCK = 4 * ROWS
NEG = -1e30
VMEM_LIMIT = 48 * 1024 * 1024
NT = (((1,), (1,)), ((), ()))


def normed(values, shift, scale):
    center = jnp.mean(values, axis=-1, keepdims=True)
    spread = jnp.mean(jnp.square(values - center), axis=-1, keepdims=True)
    unit = (values - center) * lax.rsqrt(spread + EPS)
    return (unit * (1.0 + scale) + shift).astype(jnp.bfloat16)


def head_norm(values, gain):
    factor = lax.rsqrt(jnp.mean(values * values, axis=-1, keepdims=True) + EPS)
    return (values * factor * gain).astype(jnp.bfloat16)


def dot(a, b, dims=(((1,), (0,)), ((), ()))):
    return lax.dot_general(a, b, dims, preferred_element_type=jnp.float32)


def call(kernel, args, out_shape, name, scratch=(), flops=0, moved=0, trans=0, grid=None, specs=None):
    extra = {} if grid is None else {"grid": grid, "in_specs": specs[0], "out_specs": specs[1]}
    return pl.pallas_call(
        kernel,
        out_shape=out_shape,
        scratch_shapes=list(scratch),
        compiler_params=pltpu.CompilerParams(vmem_limit_bytes=VMEM_LIMIT),
        cost_estimate=pl.CostEstimate(flops=flops, bytes_accessed=moved, transcendentals=trans),
        name=name,
        **extra,
    )(*args)


def modulate_kernel(x, mod, out):
    out[...] = normed(x[...].astype(jnp.float32), mod[0:1], mod[1:2])


def modulate(x, mod):
    shape = jax.ShapeDtypeStruct(x.shape, jnp.bfloat16)
    return call(modulate_kernel, (x, mod), shape, "modulate", moved=300_000)


def qkv_kernel(toks, w, gain, out):
    rows = toks.shape[1]
    for i in range(toks.shape[0]):
        raw = dot(toks[i], w[...], NT)
        at = slice(i * rows, (i + 1) * rows)
        out[0, at] = head_norm(raw[:, :HEAD_DIM], gain[0:1])
        out[1, at] = head_norm(raw[:, HEAD_DIM : 2 * HEAD_DIM], gain[1:2])
        out[2, at] = raw[:, 2 * HEAD_DIM :].astype(jnp.bfloat16)


def qkv(toks, w, gain):
    rows = toks.shape[0] * toks.shape[1]
    shape = jax.ShapeDtypeStruct((3, rows, HEAD_DIM), jnp.bfloat16)
    flops = 2 * rows * w.shape[0] * w.shape[1]
    return call(qkv_kernel, (toks, w, gain), shape, "qkv", flops=flops, moved=3_000_000)


def spatial_kernel(q, old, rowp, colp, out, vals_s, old_s, attn_s):
    step = pl.program_id(0)
    factor = HEAD_DIM ** (-0.5)

    @pl.when(step == 0)
    def _():
        raw = old[...].astype(jnp.float32)
        vals_s[:, :, :56] = raw[:, :56, HEAD_DIM:]
        for j in range(7):
            vals_s[:, 8 * j : 8 * j + 8, 56:72] = raw[:, 56:, 16 * j : 16 * j + 16]
        old_s[...] = raw[:, :56, :HEAD_DIM].reshape(old_s.shape).astype(jnp.bfloat16)

    at = pl.ds(pl.multiple_of(step * QBLOCK, QBLOCK), QBLOCK)
    query, key, value = q[0, at], q[1, at], q[2, at]
    old_values = vals_s[...].reshape(old_s.shape).astype(jnp.bfloat16)
    far = dot(query, old_s[...], NT)
    far = jnp.where(rowp[at] == colp[...], NEG, far)
    near = dot(query, key, NT)
    r_id = lax.broadcasted_iota(jnp.int32, (QBLOCK, QBLOCK), 0) // ROWS
    c_id = lax.broadcasted_iota(jnp.int32, (QBLOCK, QBLOCK), 1) // ROWS
    near = jnp.where(r_id == c_id, near, NEG)
    top = jnp.maximum(jnp.max(far, axis=1, keepdims=True), jnp.max(near, axis=1, keepdims=True))
    e_far = jnp.exp((far - top) * factor)
    e_near = jnp.exp((near - top) * factor)
    total = jnp.sum(e_far, axis=1, keepdims=True) + jnp.sum(e_near, axis=1, keepdims=True)
    mixed = dot(e_far.astype(jnp.bfloat16), old_values) + dot(e_near.astype(jnp.bfloat16), value)
    attn_s[...] = mixed / total
    for j in range(4):
        out[j, step] = attn_s[j * ROWS : (j + 1) * ROWS].astype(jnp.bfloat16)


def spatial(q, old, rowp, colp):
    rows = q.shape[1]
    whole = lambda a: pl.BlockSpec(a.shape, lambda i: (0,) * len(a.shape))
    out = jax.ShapeDtypeStruct((4, 4, ROWS, HEAD_DIM), jnp.bfloat16)
    args = (q, old, rowp, colp)
    specs = (
        [whole(a) for a in args],
        whole(out),
    )
    scratch = (
        pltpu.VMEM((2 * PLANE, ROWS, HEAD_DIM), jnp.float32),
        pltpu.VMEM((2 * PLANE * ROWS, HEAD_DIM), jnp.bfloat16),
        pltpu.VMEM((QBLOCK, HEAD_DIM), jnp.float32),
    )
    return call(
        spatial_kernel, args, out, "spatial", scratch, flops=600_000_000, moved=2_000_000,
        trans=1_800_000, grid=(rows // QBLOCK,), specs=specs,
    )


def heads_out_kernel(attn, w, out):
    for i in range(4):
        total = sum(dot(attn[k, i * ROWS : (i + 1) * ROWS], w[k]) for k in range(4))
        out[i] = total.astype(jnp.bfloat16)


def heads_out(attn, w):
    out = jax.ShapeDtypeStruct((4, ROWS, w.shape[2]), jnp.bfloat16)
    return call(heads_out_kernel, (attn, w), out, "heads_out", flops=150_000_000, moved=1_200_000)


def combine_kernel(part, resid, mod, middle, hmod):
    summed = part[0].astype(jnp.float32)
    for i in range(1, part.shape[0]):
        summed = summed + part[i].astype(jnp.float32)
    mid = (resid[...].astype(jnp.float32) + mod[0:1] * summed).astype(jnp.bfloat16)
    middle[...] = mid
    hmod[...] = normed(mid.astype(jnp.float32), mod[1:2], mod[2:3])


def combine(part, resid, mod):
    out = jax.ShapeDtypeStruct(resid.shape, jnp.bfloat16)
    return call(combine_kernel, (part, resid, mod), (out, out), "combine", moved=2_500_000)


def project_kernel(heads, attn, w, resid, gate, out, attn_s):
    for g in range(PLANE):
        attn_s[:, g * HEAD_DIM : (g + 1) * HEAD_DIM] = attn[heads[g]].astype(jnp.float32)
    summed = dot(attn_s[...].astype(jnp.bfloat16), w[...])
    out[...] = (resid[...].astype(jnp.float32) + gate[...] * summed).astype(jnp.bfloat16)


def project(heads, attn, w, resid, gate):
    out = jax.ShapeDtypeStruct(resid.shape, jnp.bfloat16)
    vmem = pl.BlockSpec(memory_space=pltpu.VMEM)
    specs = ([pl.BlockSpec(memory_space=pltpu.SMEM)] + [vmem] * 4, vmem)
    return call(
        project_kernel, (heads, attn, w, resid, gate), out, "project", (pltpu.VMEM(resid.shape, jnp.float32),),
        flops=150_000_000, moved=3_200_000, grid=(), specs=specs,
    )


def temporal_kernel(place, own, other, out):
    factor = HEAD_DIM ** (-0.5)
    half = own.shape[1]
    size = 2 * half * 8
    r_id = lax.broadcasted_iota(jnp.int32, (size, size), 0) % 8
    c_id = lax.broadcasted_iota(jnp.int32, (size, size), 1) % 8
    same = r_id == c_id

    for g in range(ROWS // 8):
        at = slice(8 * g, 8 * g + 8)

        def pick(i):
            return jnp.concatenate(
                [r[i, f, at].astype(jnp.float32) for r in (own, other) for f in range(half)], axis=0
            ).astype(jnp.bfloat16)

        scores = jnp.where(same, dot(pick(0), pick(1), NT), NEG)
        top = jnp.max(scores, axis=1, keepdims=True)
        expo = jnp.exp((scores - top) * factor)
        weights = (expo / jnp.sum(expo, axis=1, keepdims=True)).astype(jnp.bfloat16)
        mixed = dot(weights, pick(2)).astype(jnp.bfloat16)
        for f in range(2 * half):
            out[place[f], at] = mixed[8 * f : 8 * f + 8]


def temporal(place, own, other):
    shape = jax.ShapeDtypeStruct((2 * own.shape[1],) + own.shape[2:], jnp.bfloat16)
    vmem = pl.BlockSpec(memory_space=pltpu.VMEM)
    specs = ([pl.BlockSpec(memory_space=pltpu.SMEM), vmem, vmem], vmem)
    return call(
        temporal_kernel, (place, own, other), shape, "temporal", flops=50_000_000, moved=1_000_000,
        trans=120_000, grid=(), specs=specs,
    )


def flat(z, c, x, y, h):
    index = 0
    for value, size in zip((z, c, x, y, h), SIZES):
        index = index * size + value
    return index


def turn(z):
    return 2 * z + 8 * (z % 2)


def shifted():
    pairs = []
    for x in range(4):
        for y in range(4):
            q = 4 * x + y
            for ring in range(16):
                step = (((q + turn(ring % 8)) % 16) // 2 - ring % 8) % 8
                if step > 4 or (step == 4 and ring // 2 % 2):
                    step -= 8
                a, b = (ring + step) % 16, ring
                pairs.append((flat(a % 8, q % 2, x, y, a // 8), flat(b % 8, q % 2, x, y, b // 8)))
    return pairs


def rolled():
    return [
        [flat(z, c, q // 4, q % 4, h) for q in ((i - turn(z)) % PLANE for i in range(PLANE))]
        for z in range(8)
        for c in range(2)
        for h in range(2)
    ]


SWAP = [(0, 1), (1, 0)]


def xor_gather(block, axis):
    return [block] + [lax.ppermute(block, axis, [(i, i ^ k) for i in range(4)]) for k in (1, 2, 3)]


def line_gather(block):
    def to(part, k):
        return lax.ppermute(part, "z", [(z, z ^ k) for z in range(8)])

    far, *near = [to(block, k) for k in (4, 3, 2, 1)]
    return lax.optimization_barrier([block, *near[::-1], far] + [to(far, k) for k in (1, 2, 3)])


def local(stream, stale_keys, stale_values, modulation, w_qkv, w_out, qk_gain):
    width = stream.shape[2]
    x, y, z, c, h = [lax.axis_index(a) for a in ("x", "y", "z", "c", "h")]
    mine = y % 2 == c
    blocks = jnp.arange(16, dtype=jnp.int32)

    hmod = modulate(stream[0], modulation[0])
    toks = lax.all_gather(hmod, ("x", "y"), axis=0).reshape(4, QBLOCK, width)

    main = jnp.concatenate([stale_keys, stale_values[:, :, :56]], axis=2)
    tail = stale_values[:, :, 56:].reshape(16, 7, 8, 16).transpose(0, 2, 1, 3).reshape(16, 8, 112)
    tail = jnp.pad(tail, ((0, 0), (0, 0), (0, 16)))
    chunk = jnp.concatenate([main, tail], axis=1)
    chunk = jnp.broadcast_to(chunk[:, None], (16, 2, 64, 128)).reshape(32, 64, 128)
    old = lax.all_to_all(chunk, ("z", "c", "h"), 0, 0, tiled=True)

    rows = jnp.concatenate([w_qkv[0].reshape(3 * HEAD_DIM, width), w_out[0], w_out[1]], axis=0)
    rows = lax.ppermute(rows, AXES, shifted())
    rows = jnp.where(mine, rows, lax.ppermute(rows, "c", SWAP))
    w_col, w_head, w_last = (
        rows[: 3 * HEAD_DIM], rows[3 * HEAD_DIM : 4 * HEAD_DIM], rows[4 * HEAD_DIM :]
    )
    w_heads = lax.all_gather(w_head, "y", axis=0)
    old = lax.all_to_all(
        old.reshape(16, 2, 64, 128), AXES, 0, 0, axis_index_groups=rolled(), tiled=True
    )

    fresh = qkv(toks, w_col, qk_gain[0])
    rowp = jnp.repeat(2 * blocks + h, ROWS)[:, None]
    colp = jnp.repeat((lax.iota(jnp.int32, 2 * PLANE) - 2 * turn(z)) % (2 * PLANE), ROWS)[None, :]
    old, w_heads = lax.optimization_barrier((old, w_heads))
    attn = spatial(fresh, old.reshape(2 * PLANE, 64, 128), rowp, colp)
    attn, w_last, w_own = lax.optimization_barrier(
        (attn, w_last, w_qkv[1].reshape(3 * HEAD_DIM, width))
    )
    w_last = lax.all_gather(w_last, ("x", "y"), axis=0).reshape(width, width)
    attn = lax.all_to_all(attn, "y", 0, 0, tiled=True)
    part = heads_out(attn.reshape(4, QBLOCK, HEAD_DIM), w_heads)
    part = lax.all_to_all(part, "x", 0, 0, tiled=True)
    middle, hmod = combine(part, stream[0], jnp.concatenate([modulation[0, 2:], modulation[1, :2]]))

    toks = jnp.concatenate(line_gather(hmod), axis=0)[None]
    w_sib = lax.ppermute(w_own, "c", SWAP)
    sib = qkv(toks, w_sib, qk_gain[1])
    other = lax.ppermute(sib, "c", SWAP)
    own = qkv(toks, w_own, qk_gain[1])
    shape = (3, 8, ROWS, HEAD_DIM)
    place = 2 * (z ^ (blocks % 8)) + (c ^ (blocks // 8))
    other, w_last = lax.optimization_barrier((other, w_last))
    attn = temporal(place, own.reshape(shape), other.reshape(shape))
    attn = lax.all_to_all(attn, ("z", "c"), 0, 0, tiled=True)
    out = project((blocks + turn(z)) % 16, attn, w_last, middle, modulation[1, 2:])
    return out[None]


def solution(mesh):
    wide = Mesh(mesh.devices.reshape(SIZES), AXES)
    tm, patch = ("z", "c"), ("x", "y", "h")
    placed = (
        P(tm, patch, None),
        P(None, patch, tm),
        P(None, patch, tm),
        P(),
        P(None, None, tm, None),
        P(None, tm, None),
        P(),
    )
    return jax.shard_map(
        local, mesh=wide, in_specs=placed, out_specs=P(tm, patch, None), check_vma=False
    )
```

```python
import functools

import jax
import jax.numpy as jnp
from jax import lax
from jax.experimental import pallas as pl
from jax.experimental.pallas import tpu as pltpu
from jax.sharding import Mesh
from jax.sharding import PartitionSpec as P

HEAD_DIM = 72
EPS = 1e-06
AXES = ("z", "c", "x", "y", "h")
SIZES = (8, 2, 4, 4, 2)
ROWS = 56
PLANE = 16
QBLOCK = 4 * ROWS
NEG = -1e30
VMEM_LIMIT = 20 * 1024 * 1024
NT = (((1,), (1,)), ((), ()))


def normed(values, shift, scale):
    center = jnp.mean(values, axis=-1, keepdims=True)
    spread = jnp.mean(jnp.square(values - center), axis=-1, keepdims=True)
    unit = (values - center) * lax.rsqrt(spread + EPS)
    return (unit * (1.0 + scale) + shift).astype(jnp.bfloat16)


def head_norm(values, gain):
    factor = lax.rsqrt(jnp.mean(values * values, axis=-1, keepdims=True) + EPS)
    return (values * factor * gain).astype(jnp.bfloat16)


def dot(a, b, dims=(((1,), (0,)), ((), ()))):
    return lax.dot_general(a, b, dims, preferred_element_type=jnp.float32)


def call(kernel, args, out_shape, name, scratch=(), flops=0, moved=0, trans=0, grid=None, specs=None):
    extra = {} if grid is None else {"grid": grid, "in_specs": specs[0], "out_specs": specs[1]}
    return pl.pallas_call(
        kernel,
        out_shape=out_shape,
        scratch_shapes=list(scratch),
        compiler_params=pltpu.CompilerParams(vmem_limit_bytes=VMEM_LIMIT),
        cost_estimate=pl.CostEstimate(flops=flops, bytes_accessed=moved, transcendentals=trans),
        name=name,
        **extra,
    )(*args)


def modulate_kernel(x, mod, out):
    out[...] = normed(x[...].astype(jnp.float32), mod[0:1], mod[1:2])


def modulate(x, mod):
    shape = jax.ShapeDtypeStruct(x.shape, jnp.bfloat16)
    return call(modulate_kernel, (x, mod), shape, "modulate", moved=300_000)


def pack_kernel(keys, values, out, scratch):
    old = values[...].astype(jnp.float32)
    scratch[:, :ROWS, :HEAD_DIM] = keys[...].astype(jnp.float32)
    scratch[:, :ROWS, HEAD_DIM:] = old[:, :, :56]
    scratch[:, ROWS:] = jnp.zeros_like(scratch[:, ROWS:])
    for j in range(7):
        scratch[:, ROWS:, 16 * j : 16 * j + 16] = old[:, 8 * j : 8 * j + 8, 56:]
    chunk = scratch[...].astype(jnp.bfloat16)
    for i in range(2):
        out[:, i] = chunk


def pack(keys, values):
    frames, step = keys.shape[0], 4
    out = jax.ShapeDtypeStruct((frames, 2, 64, 128), jnp.bfloat16)
    block = pl.BlockSpec((step, ROWS, HEAD_DIM), lambda i: (i, 0, 0))
    specs = ([block, block], pl.BlockSpec((step, 2, 64, 128), lambda i: (i, 0, 0, 0)))
    packed = call(
        pack_kernel, (keys, values), out, "pack", (pltpu.VMEM((step, 64, 128), jnp.float32),),
        moved=1_000_000, grid=(frames // step,), specs=specs,
    )
    return packed.reshape(2 * frames, 64, 128)


def qkv_kernel(toks, w, gain, out):
    rows = toks.shape[1]
    for i in range(toks.shape[0]):
        raw = dot(toks[i], w[...], NT)
        at = slice(i * rows, (i + 1) * rows)
        out[0, at] = head_norm(raw[:, :HEAD_DIM], gain[0:1])
        out[1, at] = head_norm(raw[:, HEAD_DIM : 2 * HEAD_DIM], gain[1:2])
        out[2, at] = raw[:, 2 * HEAD_DIM :].astype(jnp.bfloat16)


def qkv(toks, w, gain):
    rows = toks.shape[0] * toks.shape[1]
    shape = jax.ShapeDtypeStruct((3, rows, HEAD_DIM), jnp.bfloat16)
    flops = 2 * rows * w.shape[0] * w.shape[1]
    return call(qkv_kernel, (toks, w, gain), shape, "qkv", flops=flops, moved=3_000_000)


def spatial_kernel(q, old, rowp, colp, out, vals_s, old_s, attn_s):
    step = pl.program_id(0)
    factor = HEAD_DIM ** (-0.5)

    @pl.when(step == 0)
    def _():
        raw = old[...].astype(jnp.float32)
        vals_s[:, :, :56] = raw[:, :56, HEAD_DIM:]
        for j in range(7):
            vals_s[:, 8 * j : 8 * j + 8, 56:72] = raw[:, 56:, 16 * j : 16 * j + 16]
        old_s[...] = raw[:, :56, :HEAD_DIM].reshape(old_s.shape).astype(jnp.bfloat16)

    at = pl.ds(pl.multiple_of(step * QBLOCK, QBLOCK), QBLOCK)
    query, key, value = q[0, at], q[1, at], q[2, at]
    old_values = vals_s[...].reshape(old_s.shape).astype(jnp.bfloat16)
    far = dot(query, old_s[...], NT)
    far = jnp.where(rowp[at] == colp[...], NEG, far)
    near = dot(query, key, NT)
    r_id = lax.broadcasted_iota(jnp.int32, (QBLOCK, QBLOCK), 0) // ROWS
    c_id = lax.broadcasted_iota(jnp.int32, (QBLOCK, QBLOCK), 1) // ROWS
    near = jnp.where(r_id == c_id, near, NEG)
    top = jnp.maximum(jnp.max(far, axis=1, keepdims=True), jnp.max(near, axis=1, keepdims=True))
    e_far = jnp.exp((far - top) * factor)
    e_near = jnp.exp((near - top) * factor)
    total = jnp.sum(e_far, axis=1, keepdims=True) + jnp.sum(e_near, axis=1, keepdims=True)
    mixed = dot(e_far.astype(jnp.bfloat16), old_values) + dot(e_near.astype(jnp.bfloat16), value)
    attn_s[...] = mixed / total
    for j in range(4):
        out[j, step] = attn_s[j * ROWS : (j + 1) * ROWS].astype(jnp.bfloat16)


def spatial(q, old, rowp, colp):
    rows = q.shape[1]
    whole = lambda a: pl.BlockSpec(a.shape, lambda i: (0,) * len(a.shape))
    out = jax.ShapeDtypeStruct((4, 4, ROWS, HEAD_DIM), jnp.bfloat16)
    args = (q, old, rowp, colp)
    specs = (
        [whole(a) for a in args],
        whole(out),
    )
    scratch = (
        pltpu.VMEM((2 * PLANE, ROWS, HEAD_DIM), jnp.float32),
        pltpu.VMEM((2 * PLANE * ROWS, HEAD_DIM), jnp.bfloat16),
        pltpu.VMEM((QBLOCK, HEAD_DIM), jnp.float32),
    )
    return call(
        spatial_kernel, args, out, "spatial", scratch, flops=600_000_000, moved=2_000_000,
        trans=1_800_000, grid=(rows // QBLOCK,), specs=specs,
    )


def heads_out_kernel(place, attn, w0, w1, w2, w3, out):
    for i in range(4):
        total = sum(dot(attn[place[k], i * ROWS : (i + 1) * ROWS], w[w.shape[0] - HEAD_DIM :]) for k, w in enumerate((w0, w1, w2, w3)))
        out[i] = total.astype(jnp.bfloat16)


def heads_out(place, attn, ws):
    out = jax.ShapeDtypeStruct((4, ROWS, ws[0].shape[1]), jnp.bfloat16)
    vmem = pl.BlockSpec(memory_space=pltpu.VMEM)
    specs = ([pl.BlockSpec(memory_space=pltpu.SMEM)] + [vmem] * 5, vmem)
    return call(
        heads_out_kernel, (place, attn, *ws), out, "heads_out", flops=150_000_000, moved=1_200_000,
        grid=(), specs=specs,
    )


def combine_kernel(part, resid, mod, middle, hmod):
    summed = part[0].astype(jnp.float32)
    for i in range(1, part.shape[0]):
        summed = summed + part[i].astype(jnp.float32)
    mid = (resid[...].astype(jnp.float32) + mod[0:1] * summed).astype(jnp.bfloat16)
    middle[...] = mid
    hmod[...] = normed(mid.astype(jnp.float32), mod[1:2], mod[2:3])


def combine(part, resid, mod):
    out = jax.ShapeDtypeStruct(resid.shape, jnp.bfloat16)
    return call(combine_kernel, (part, resid, mod), (out, out), "combine", moved=2_500_000)


def project_kernel(heads, attn, w, resid, gate, out, attn_s):
    @pl.when(pl.program_id(0) == 0)
    def _():
        for g in range(PLANE):
            piece = attn[heads[g]].astype(jnp.float32)
            at = g * HEAD_DIM
            attn_s[:32, at : at + 72] = piece[:, :72]
            attn_s[32:, at : at + 56] = piece[:24, 72:]
            for j in range(3):
                attn_s[32 + 8 * j : 40 + 8 * j, at + 56 : at + 72] = piece[24:, 72 + 16 * j : 88 + 16 * j]

    summed = dot(attn_s[...].astype(jnp.bfloat16), w[...])
    out[...] = (resid[...].astype(jnp.float32) + gate[...] * summed).astype(jnp.bfloat16)


def project(heads, attn, w, resid, gate):
    out = jax.ShapeDtypeStruct(resid.shape, jnp.bfloat16)
    part = w.shape[1] // 3
    columns = lambda a: pl.BlockSpec((a.shape[0], part), lambda i: (0, i))
    specs = (
        [
            pl.BlockSpec(memory_space=pltpu.SMEM),
            pl.BlockSpec(attn.shape, lambda i: (0, 0, 0)),
            columns(w), columns(resid), columns(gate),
        ],
        columns(resid),
    )
    return call(
        project_kernel, (heads, attn, w, resid, gate), out, "project", (pltpu.VMEM(resid.shape, jnp.float32),),
        flops=150_000_000, moved=3_200_000, grid=(3,), specs=specs,
    )


def temporal_kernel(place, own, other, out, packed):
    factor = HEAD_DIM ** (-0.5)
    half = own.shape[1]
    size = 2 * half * 8
    r_id = lax.broadcasted_iota(jnp.int32, (size, size), 0) % 8
    c_id = lax.broadcasted_iota(jnp.int32, (size, size), 1) % 8
    same = r_id == c_id

    for g in range(ROWS // 8):
        at = slice(8 * g, 8 * g + 8)

        def pick(i):
            return jnp.concatenate(
                [r[i, f, at].astype(jnp.float32) for r in (own, other) for f in range(half)], axis=0
            ).astype(jnp.bfloat16)

        scores = jnp.where(same, dot(pick(0), pick(1), NT), NEG)
        top = jnp.max(scores, axis=1, keepdims=True)
        expo = jnp.exp((scores - top) * factor)
        weights = (expo / jnp.sum(expo, axis=1, keepdims=True)).astype(jnp.bfloat16)
        mixed = dot(weights, pick(2)).reshape(2 * half, 8, HEAD_DIM)
        if g < 4:
            packed[:, at, :72] = mixed
        else:
            packed[:, slice(8 * g - 32, 8 * g - 24), 72:] = mixed[:, :, :56]
            packed[:, 24:, 72 + 16 * (g - 4) : 88 + 16 * (g - 4)] = mixed[:, :, 56:]

    packed[:, 24:, 120:] = jnp.zeros_like(packed[:, 24:, 120:])
    for f in range(2 * half):
        out[place[f]] = packed[f].astype(jnp.bfloat16)


def temporal(place, own, other):
    frames = 2 * own.shape[1]
    shape = jax.ShapeDtypeStruct((frames, 32, 128), jnp.bfloat16)
    vmem = pl.BlockSpec(memory_space=pltpu.VMEM)
    specs = ([pl.BlockSpec(memory_space=pltpu.SMEM), vmem, vmem], vmem)
    return call(
        temporal_kernel, (place, own, other), shape, "temporal", (pltpu.VMEM((frames, 32, 128), jnp.float32),),
        flops=50_000_000, moved=1_000_000, trans=120_000, grid=(), specs=specs,
    )


def flat(z, c, x, y, h):
    index = 0
    for value, size in zip((z, c, x, y, h), SIZES):
        index = index * size + value
    return index


def turn(z):
    return 2 * z + 8 * (z % 2)


def shifted():
    pairs = []
    for x in range(4):
        for y in range(4):
            q = 4 * x + y
            for ring in range(16):
                step = (((q + turn(ring % 8)) % 16) // 2 - ring % 8) % 8
                if step > 4 or (step == 4 and ring // 2 % 2):
                    step -= 8
                a, b = (ring + step) % 16, ring
                pairs.append((flat(a % 8, q % 2, x, y, a // 8), flat(b % 8, q % 2, x, y, b // 8)))
    return pairs


def rolled():
    return [
        [flat(z, c, q // 4, q % 4, h) for q in ((i - turn(z)) % PLANE for i in range(PLANE))]
        for z in range(8)
        for c in range(2)
        for h in range(2)
    ]


SWAP = [(0, 1), (1, 0)]


def xor_gather(block, axis):
    return [block] + [lax.ppermute(block, axis, [(i, i ^ k) for i in range(4)]) for k in (1, 2, 3)]


def xor_gather(block, axis):
    return [block] + [lax.ppermute(block, axis, [(i, i ^ k) for i in range(4)]) for k in (1, 2, 3)]


LOOP = (0, 2, 4, 6, 7, 5, 3, 1)


def line_gather(block):
    return lax.all_gather(block, "z", axis=0, axis_index_groups=[list(LOOP)])


def local(stream, stale_keys, stale_values, modulation, w_qkv, w_out, qk_gain):
    width = stream.shape[2]
    x, y, z, c, h = [lax.axis_index(a) for a in ("x", "y", "z", "c", "h")]
    mine = y % 2 == c
    blocks = jnp.arange(16, dtype=jnp.int32)

    hmod = modulate(stream[0], modulation[0])
    toks = lax.all_gather(hmod, ("x", "y"), axis=0).reshape(4, QBLOCK, width)

    chunk = pack(stale_keys, stale_values)
    old = lax.all_to_all(chunk, ("z", "c", "h"), 0, 0, tiled=True)

    rows = jnp.concatenate([w_qkv[0].reshape(3 * HEAD_DIM, width), w_out[0], w_out[1]], axis=0)
    rows = lax.ppermute(rows, AXES, shifted())
    rows = jnp.where(mine, rows, lax.ppermute(rows, "c", SWAP))
    w_col, w_head, w_last = (
        rows[: 3 * HEAD_DIM], rows[3 * HEAD_DIM : 4 * HEAD_DIM], rows[4 * HEAD_DIM :]
    )
    old = lax.all_to_all(
        old.reshape(16, 2, 64, 128), AXES, 0, 0, axis_index_groups=rolled(), tiled=True
    )

    fresh = qkv(toks, w_col, qk_gain[0])
    rowp = jnp.repeat(2 * blocks + h, ROWS)[:, None]
    colp = jnp.repeat((lax.iota(jnp.int32, 2 * PLANE) - 2 * turn(z)) % (2 * PLANE), ROWS)[None, :]
    w_heads = xor_gather(rows[3 * HEAD_DIM - 0 : 4 * HEAD_DIM], "y")
    attn = spatial(fresh, old.reshape(2 * PLANE, 64, 128), rowp, colp)
    attn, w_heads, w_last, w_own = lax.optimization_barrier(
        (attn, w_heads, w_last, w_qkv[1].reshape(3 * HEAD_DIM, width))
    )
    w_last = lax.all_gather(w_last, ("x", "y"), axis=0).reshape(width, width)
    attn = lax.all_to_all(attn, "y", 0, 0, tiled=True)
    part = heads_out(y ^ blocks[:4], attn.reshape(4, QBLOCK, HEAD_DIM), w_heads)
    part = lax.all_to_all(part, "x", 0, 0, tiled=True)
    middle, hmod = combine(part, stream[0], jnp.concatenate([modulation[0, 2:], modulation[1, :2]]))

    toks = line_gather(hmod).reshape(1, 8 * ROWS, width)
    w_sib = lax.ppermute(w_own, "c", SWAP)
    sib = qkv(toks, w_sib, qk_gain[1])
    other = lax.ppermute(sib, "c", SWAP)
    own = qkv(toks, w_own, qk_gain[1])
    shape = (3, 8, ROWS, HEAD_DIM)
    place = 2 * jnp.array(LOOP * 2, jnp.int32) + (c ^ (blocks // 8))
    other, w_last = lax.optimization_barrier((other, w_last))
    attn = temporal(place, own.reshape(shape), other.reshape(shape))
    attn = lax.all_to_all(attn, ("z", "c"), 0, 0, tiled=True)
    out = project((blocks + turn(z)) % 16, attn, w_last, middle, modulation[1, 2:])
    return out[None]


def solution(mesh):
    wide = Mesh(mesh.devices.reshape(SIZES), AXES)
    tm, patch = ("z", "c"), ("x", "y", "h")
    placed = (
        P(tm, patch, None),
        P(None, patch, tm),
        P(None, patch, tm),
        P(),
        P(None, None, tm, None),
        P(None, tm, None),
        P(),
    )
    return jax.shard_map(
        local, mesh=wide, in_specs=placed, out_specs=P(tm, patch, None), check_vma=False
    )
```

```python
import functools

import jax
import jax.numpy as jnp
from jax import lax
from jax.experimental import pallas as pl
from jax.experimental.pallas import tpu as pltpu
from jax.sharding import Mesh
from jax.sharding import PartitionSpec as P

HEAD_DIM = 72
EPS = 1e-06
AXES = ("z", "c", "x", "y", "h")
SIZES = (8, 2, 4, 4, 2)
ROWS = 56
PLANE = 16
QBLOCK = 4 * ROWS
NEG = -1e30
VMEM_LIMIT = 20 * 1024 * 1024
VMEM_ALL = 60 * 1024 * 1024
NT = (((1,), (1,)), ((), ()))


def normed(values, shift, scale):
    center = jnp.mean(values, axis=-1, keepdims=True)
    spread = jnp.mean(jnp.square(values - center), axis=-1, keepdims=True)
    unit = (values - center) * lax.rsqrt(spread + EPS)
    return (unit * (1.0 + scale) + shift).astype(jnp.bfloat16)


def head_norm(values, gain):
    factor = lax.rsqrt(jnp.mean(values * values, axis=-1, keepdims=True) + EPS)
    return (values * factor * gain).astype(jnp.bfloat16)


def dot(a, b, dims=(((1,), (0,)), ((), ()))):
    return lax.dot_general(a, b, dims, preferred_element_type=jnp.float32)


def call(
    kernel, args, out_shape, name, scratch=(), flops=0, moved=0, trans=0, grid=None, specs=None, limit=VMEM_LIMIT
):
    extra = {} if grid is None else {"grid": grid, "in_specs": specs[0], "out_specs": specs[1]}
    return pl.pallas_call(
        kernel,
        out_shape=out_shape,
        scratch_shapes=list(scratch),
        compiler_params=pltpu.CompilerParams(vmem_limit_bytes=limit),
        cost_estimate=pl.CostEstimate(flops=flops, bytes_accessed=moved, transcendentals=trans),
        name=name,
        **extra,
    )(*args)


def modulate_kernel(x, mod, out):
    out[...] = normed(x[...].astype(jnp.float32), mod[0:1], mod[1:2])


def modulate(x, mod):
    shape = jax.ShapeDtypeStruct(x.shape, jnp.bfloat16)
    return call(modulate_kernel, (x, mod), shape, "modulate", moved=300_000)


def pack_kernel(keys, values, out, scratch):
    old = values[...].astype(jnp.float32)
    scratch[:, :ROWS, :HEAD_DIM] = keys[...].astype(jnp.float32)
    scratch[:, :ROWS, HEAD_DIM:] = old[:, :, :56]
    scratch[:, ROWS:] = jnp.zeros_like(scratch[:, ROWS:])
    for j in range(7):
        scratch[:, ROWS:, 16 * j : 16 * j + 16] = old[:, 8 * j : 8 * j + 8, 56:]
    chunk = scratch[...].astype(jnp.bfloat16)
    for i in range(2):
        out[:, i] = chunk


def pack(keys, values):
    frames, step = keys.shape[0], 4
    out = jax.ShapeDtypeStruct((frames, 2, 64, 128), jnp.bfloat16)
    block = pl.BlockSpec((step, ROWS, HEAD_DIM), lambda i: (i, 0, 0))
    specs = ([block, block], pl.BlockSpec((step, 2, 64, 128), lambda i: (i, 0, 0, 0)))
    packed = call(
        pack_kernel, (keys, values), out, "pack", (pltpu.VMEM((step, 64, 128), jnp.float32),),
        moved=1_000_000, grid=(frames // step,), specs=specs,
    )
    return packed.reshape(2 * frames, 64, 128)


def qkv_kernel(toks, w, gain, out):
    rows = toks.shape[1]
    for i in range(toks.shape[0]):
        raw = dot(toks[i], w[...], NT)
        at = slice(i * rows, (i + 1) * rows)
        out[0, at] = head_norm(raw[:, :HEAD_DIM], gain[0:1])
        out[1, at] = head_norm(raw[:, HEAD_DIM : 2 * HEAD_DIM], gain[1:2])
        out[2, at] = raw[:, 2 * HEAD_DIM :].astype(jnp.bfloat16)


def qkv(toks, w, gain):
    rows = toks.shape[0] * toks.shape[1]
    shape = jax.ShapeDtypeStruct((3, rows, HEAD_DIM), jnp.bfloat16)
    flops = 2 * rows * w.shape[0] * w.shape[1]
    return call(qkv_kernel, (toks, w, gain), shape, "qkv", flops=flops, moved=3_000_000)


def spatial_kernel(q, old, rowp, colp, out, vals_s, old_s, attn_s):
    step = pl.program_id(0)
    factor = HEAD_DIM ** (-0.5)

    @pl.when(step == 0)
    def _():
        raw = old[...].astype(jnp.float32)
        vals_s[:, :, :56] = raw[:, :56, HEAD_DIM:]
        for j in range(7):
            vals_s[:, 8 * j : 8 * j + 8, 56:72] = raw[:, 56:, 16 * j : 16 * j + 16]
        old_s[...] = raw[:, :56, :HEAD_DIM].reshape(old_s.shape).astype(jnp.bfloat16)

    at = pl.ds(pl.multiple_of(step * QBLOCK, QBLOCK), QBLOCK)
    query, key, value = q[0, at], q[1, at], q[2, at]
    old_values = vals_s[...].reshape(old_s.shape).astype(jnp.bfloat16)
    far = dot(query, old_s[...], NT)
    far = jnp.where(rowp[at] == colp[...], NEG, far)
    near = dot(query, key, NT)
    r_id = lax.broadcasted_iota(jnp.int32, (QBLOCK, QBLOCK), 0) // ROWS
    c_id = lax.broadcasted_iota(jnp.int32, (QBLOCK, QBLOCK), 1) // ROWS
    near = jnp.where(r_id == c_id, near, NEG)
    top = jnp.maximum(jnp.max(far, axis=1, keepdims=True), jnp.max(near, axis=1, keepdims=True))
    e_far = jnp.exp((far - top) * factor)
    e_near = jnp.exp((near - top) * factor)
    total = jnp.sum(e_far, axis=1, keepdims=True) + jnp.sum(e_near, axis=1, keepdims=True)
    mixed = dot(e_far.astype(jnp.bfloat16), old_values) + dot(e_near.astype(jnp.bfloat16), value)
    attn_s[...] = mixed / total
    for j in range(4):
        out[j, step] = attn_s[j * ROWS : (j + 1) * ROWS].astype(jnp.bfloat16)


def spatial(q, old, rowp, colp):
    rows = q.shape[1]
    whole = lambda a: pl.BlockSpec(a.shape, lambda i: (0,) * len(a.shape))
    out = jax.ShapeDtypeStruct((4, 4, ROWS, HEAD_DIM), jnp.bfloat16)
    args = (q, old, rowp, colp)
    specs = (
        [whole(a) for a in args],
        whole(out),
    )
    scratch = (
        pltpu.VMEM((2 * PLANE, ROWS, HEAD_DIM), jnp.float32),
        pltpu.VMEM((2 * PLANE * ROWS, HEAD_DIM), jnp.bfloat16),
        pltpu.VMEM((QBLOCK, HEAD_DIM), jnp.float32),
    )
    return call(
        spatial_kernel, args, out, "spatial", scratch, flops=600_000_000, moved=2_000_000,
        trans=1_800_000, grid=(rows // QBLOCK,), specs=specs,
    )


def heads_out_kernel(place, attn, w0, w1, w2, w3, out):
    for i in range(4):
        total = sum(dot(attn[place[k], i * ROWS : (i + 1) * ROWS], w[w.shape[0] - HEAD_DIM :]) for k, w in enumerate((w0, w1, w2, w3)))
        out[i] = total.astype(jnp.bfloat16)


def heads_out(place, attn, ws):
    out = jax.ShapeDtypeStruct((4, ROWS, ws[0].shape[1]), jnp.bfloat16)
    vmem = pl.BlockSpec(memory_space=pltpu.VMEM)
    specs = ([pl.BlockSpec(memory_space=pltpu.SMEM)] + [vmem] * 5, vmem)
    return call(
        heads_out_kernel, (place, attn, *ws), out, "heads_out", flops=150_000_000, moved=1_200_000,
        grid=(), specs=specs,
    )


def combine_kernel(part, resid, mod, middle, hmod):
    summed = part[0].astype(jnp.float32)
    for i in range(1, part.shape[0]):
        summed = summed + part[i].astype(jnp.float32)
    mid = (resid[...].astype(jnp.float32) + mod[0:1] * summed).astype(jnp.bfloat16)
    middle[...] = mid
    hmod[...] = normed(mid.astype(jnp.float32), mod[1:2], mod[2:3])


def combine(part, resid, mod):
    out = jax.ShapeDtypeStruct(resid.shape, jnp.bfloat16)
    return call(combine_kernel, (part, resid, mod), (out, out), "combine", moved=2_500_000)


def project_kernel(heads, attn, w, resid, gate, out, attn_s, w_s, sems):
    part = w.shape[0] // 3
    pieces = [pl.ds(i * part, part) for i in range(3)]
    copies = [pltpu.make_async_copy(w.at[at], w_s.at[at], sems.at[i]) for i, at in enumerate(pieces)]
    for copy in copies:
        copy.start()
    for g in range(PLANE):
        piece = attn[heads[g]].astype(jnp.float32)
        at = g * HEAD_DIM
        attn_s[:32, at : at + 72] = piece[:, :72]
        attn_s[32:, at : at + 56] = piece[:24, 72:]
        for j in range(3):
            attn_s[32 + 8 * j : 40 + 8 * j, at + 56 : at + 72] = piece[24:, 72 + 16 * j : 88 + 16 * j]
    summed = jnp.zeros(out.shape, jnp.float32)
    for copy, at in zip(copies, pieces):
        copy.wait()
        summed = summed + dot(attn_s[:, at].astype(jnp.bfloat16), w_s[at])
    out[...] = (resid[...].astype(jnp.float32) + gate[...] * summed).astype(jnp.bfloat16)


def project(heads, attn, w, resid, gate):
    out = jax.ShapeDtypeStruct(resid.shape, jnp.bfloat16)
    vmem = pl.BlockSpec(memory_space=pltpu.VMEM)
    specs = (
        [pl.BlockSpec(memory_space=pltpu.SMEM), vmem, pl.BlockSpec(memory_space=pl.ANY), vmem, vmem],
        vmem,
    )
    scratch = (
        pltpu.VMEM(resid.shape, jnp.float32),
        pltpu.VMEM(w.shape, w.dtype),
        pltpu.SemaphoreType.DMA((3,)),
    )
    return call(
        project_kernel, (heads, attn, w, resid, gate), out, "project", scratch, flops=150_000_000,
        moved=3_200_000, grid=(), specs=specs, limit=VMEM_ALL,
    )


def temporal_kernel(place, own, other, out, packed):
    factor = HEAD_DIM ** (-0.5)
    half = own.shape[1]
    size = 2 * half * 8
    r_id = lax.broadcasted_iota(jnp.int32, (size, size), 0) % 8
    c_id = lax.broadcasted_iota(jnp.int32, (size, size), 1) % 8
    same = r_id == c_id

    for g in range(ROWS // 8):
        at = slice(8 * g, 8 * g + 8)

        def pick(i):
            return jnp.concatenate(
                [r[i, f, at].astype(jnp.float32) for r in (own, other) for f in range(half)], axis=0
            ).astype(jnp.bfloat16)

        scores = jnp.where(same, dot(pick(0), pick(1), NT), NEG)
        top = jnp.max(scores, axis=1, keepdims=True)
        expo = jnp.exp((scores - top) * factor)
        weights = (expo / jnp.sum(expo, axis=1, keepdims=True)).astype(jnp.bfloat16)
        mixed = dot(weights, pick(2)).reshape(2 * half, 8, HEAD_DIM)
        if g < 4:
            packed[:, at, :72] = mixed
        else:
            packed[:, slice(8 * g - 32, 8 * g - 24), 72:] = mixed[:, :, :56]
            packed[:, 24:, 72 + 16 * (g - 4) : 88 + 16 * (g - 4)] = mixed[:, :, 56:]

    packed[:, 24:, 120:] = jnp.zeros_like(packed[:, 24:, 120:])
    for f in range(2 * half):
        out[place[f]] = packed[f].astype(jnp.bfloat16)


def temporal(place, own, other):
    frames = 2 * own.shape[1]
    shape = jax.ShapeDtypeStruct((frames, 32, 128), jnp.bfloat16)
    vmem = pl.BlockSpec(memory_space=pltpu.VMEM)
    specs = ([pl.BlockSpec(memory_space=pltpu.SMEM), vmem, vmem], vmem)
    return call(
        temporal_kernel, (place, own, other), shape, "temporal", (pltpu.VMEM((frames, 32, 128), jnp.float32),),
        flops=50_000_000, moved=1_000_000, trans=120_000, grid=(), specs=specs,
    )


def flat(z, c, x, y, h):
    index = 0
    for value, size in zip((z, c, x, y, h), SIZES):
        index = index * size + value
    return index


def turn(z):
    return 2 * z + 8 * (z % 2)


def shifted():
    pairs = []
    for x in range(4):
        for y in range(4):
            q = 4 * x + y
            for ring in range(16):
                step = (((q + turn(ring % 8)) % 16) // 2 - ring % 8) % 8
                if step > 4 or (step == 4 and ring // 2 % 2):
                    step -= 8
                a, b = (ring + step) % 16, ring
                pairs.append((flat(a % 8, q % 2, x, y, a // 8), flat(b % 8, q % 2, x, y, b // 8)))
    return pairs


def rolled():
    return [
        [flat(z, c, q // 4, q % 4, h) for q in ((i - turn(z)) % PLANE for i in range(PLANE))]
        for z in range(8)
        for c in range(2)
        for h in range(2)
    ]


SWAP = [(0, 1), (1, 0)]


def xor_gather(block, axis):
    return [block] + [lax.ppermute(block, axis, [(i, i ^ k) for i in range(4)]) for k in (1, 2, 3)]


def xor_gather(block, axis):
    return [block] + [lax.ppermute(block, axis, [(i, i ^ k) for i in range(4)]) for k in (1, 2, 3)]


LOOP = (0, 2, 4, 6, 7, 5, 3, 1)


def line_gather(block):
    return lax.all_gather(block, "z", axis=0, axis_index_groups=[list(LOOP)])


def local(stream, stale_keys, stale_values, modulation, w_qkv, w_out, qk_gain):
    width = stream.shape[2]
    x, y, z, c, h = [lax.axis_index(a) for a in ("x", "y", "z", "c", "h")]
    mine = y % 2 == c
    blocks = jnp.arange(16, dtype=jnp.int32)

    hmod = modulate(stream[0], modulation[0])
    toks = lax.all_gather(hmod, ("x", "y"), axis=0).reshape(4, QBLOCK, width)

    chunk = pack(stale_keys, stale_values)
    old = lax.all_to_all(chunk, ("z", "c", "h"), 0, 0, tiled=True)

    rows = jnp.concatenate([w_qkv[0].reshape(3 * HEAD_DIM, width), w_out[0], w_out[1]], axis=0)
    rows = lax.ppermute(rows, AXES, shifted())
    rows = jnp.where(mine, rows, lax.ppermute(rows, "c", SWAP))
    w_col, w_head, w_last = (
        rows[: 3 * HEAD_DIM], rows[3 * HEAD_DIM : 4 * HEAD_DIM], rows[4 * HEAD_DIM :]
    )
    old = lax.all_to_all(
        old.reshape(16, 2, 64, 128), AXES, 0, 0, axis_index_groups=rolled(), tiled=True
    )

    fresh = qkv(toks, w_col, qk_gain[0])
    rowp = jnp.repeat(2 * blocks + h, ROWS)[:, None]
    colp = jnp.repeat((lax.iota(jnp.int32, 2 * PLANE) - 2 * turn(z)) % (2 * PLANE), ROWS)[None, :]
    w_heads = xor_gather(rows[3 * HEAD_DIM - 0 : 4 * HEAD_DIM], "y")
    attn = spatial(fresh, old.reshape(2 * PLANE, 64, 128), rowp, colp)
    attn, w_heads = lax.optimization_barrier((attn, w_heads))
    attn = lax.all_to_all(attn, "y", 0, 0, tiled=True)
    attn, w_last, w_own = lax.optimization_barrier(
        (attn, w_last, w_qkv[1].reshape(3 * HEAD_DIM, width))
    )
    w_last = lax.all_gather(w_last, ("x", "y"), axis=0).reshape(width, width)
    part = heads_out(y ^ blocks[:4], attn.reshape(4, QBLOCK, HEAD_DIM), w_heads)
    part = lax.all_to_all(part, "x", 0, 0, tiled=True)
    middle, hmod = combine(part, stream[0], jnp.concatenate([modulation[0, 2:], modulation[1, :2]]))

    toks = line_gather(hmod).reshape(1, 8 * ROWS, width)
    w_sib = lax.ppermute(w_own, "c", SWAP)
    sib = qkv(toks, w_sib, qk_gain[1])
    other = lax.ppermute(sib, "c", SWAP)
    own = qkv(toks, w_own, qk_gain[1])
    shape = (3, 8, ROWS, HEAD_DIM)
    place = 2 * jnp.array(LOOP * 2, jnp.int32) + (c ^ (blocks // 8))
    attn = temporal(place, own.reshape(shape), other.reshape(shape))
    attn = lax.all_to_all(attn, ("z", "c"), 0, 0, tiled=True)
    out = project((blocks + turn(z)) % 16, attn, w_last, middle, modulation[1, 2:])
    return out[None]


def solution(mesh):
    wide = Mesh(mesh.devices.reshape(SIZES), AXES)
    tm, patch = ("z", "c"), ("x", "y", "h")
    placed = (
        P(tm, patch, None),
        P(None, patch, tm),
        P(None, patch, tm),
        P(),
        P(None, None, tm, None),
        P(None, tm, None),
        P(),
    )
    return jax.shard_map(
        local, mesh=wide, in_specs=placed, out_specs=P(tm, patch, None), check_vma=False
    )
```

```python
import functools

import jax
import jax.numpy as jnp
from jax import lax
from jax.experimental import pallas as pl
from jax.experimental.pallas import tpu as pltpu
from jax.sharding import Mesh
from jax.sharding import PartitionSpec as P

HEAD_DIM = 72
EPS = 1e-06
AXES = ("z", "c", "x", "y", "h")
SIZES = (8, 2, 4, 4, 2)
ROWS = 56
PLANE = 16
QBLOCK = 4 * ROWS
NEG = -1e30
VMEM_LIMIT = 20 * 1024 * 1024
VMEM_ALL = 60 * 1024 * 1024
NT = (((1,), (1,)), ((), ()))


def normed(values, shift, scale):
    center = jnp.mean(values, axis=-1, keepdims=True)
    spread = jnp.mean(jnp.square(values - center), axis=-1, keepdims=True)
    unit = (values - center) * lax.rsqrt(spread + EPS)
    return (unit * (1.0 + scale) + shift).astype(jnp.bfloat16)


def head_norm(values, gain):
    factor = lax.rsqrt(jnp.mean(values * values, axis=-1, keepdims=True) + EPS)
    return (values * factor * gain).astype(jnp.bfloat16)


def dot(a, b, dims=(((1,), (0,)), ((), ()))):
    return lax.dot_general(a, b, dims, preferred_element_type=jnp.float32)


def call(
    kernel, args, out_shape, name, scratch=(), flops=0, moved=0, trans=0, grid=None, specs=None, limit=VMEM_LIMIT
):
    extra = {} if grid is None else {"grid": grid, "in_specs": specs[0], "out_specs": specs[1]}
    return pl.pallas_call(
        kernel,
        out_shape=out_shape,
        scratch_shapes=list(scratch),
        compiler_params=pltpu.CompilerParams(vmem_limit_bytes=limit),
        cost_estimate=pl.CostEstimate(flops=flops, bytes_accessed=moved, transcendentals=trans),
        name=name,
        **extra,
    )(*args)


def modulate_kernel(x, mod, out):
    out[...] = normed(x[...].astype(jnp.float32), mod[0:1], mod[1:2])


def modulate(x, mod):
    shape = jax.ShapeDtypeStruct(x.shape, jnp.bfloat16)
    return call(modulate_kernel, (x, mod), shape, "modulate", moved=300_000)


def pack_kernel(keys, values, out, scratch):
    old = values[...].astype(jnp.float32)
    scratch[:, :ROWS, :HEAD_DIM] = keys[...].astype(jnp.float32)
    scratch[:, :ROWS, HEAD_DIM:] = old[:, :, :56]
    scratch[:, ROWS:] = jnp.zeros_like(scratch[:, ROWS:])
    for j in range(7):
        scratch[:, ROWS:, 16 * j : 16 * j + 16] = old[:, 8 * j : 8 * j + 8, 56:]
    chunk = scratch[...].astype(jnp.bfloat16)
    for i in range(2):
        out[:, i] = chunk


def pack(keys, values):
    frames, step = keys.shape[0], 4
    out = jax.ShapeDtypeStruct((frames, 2, 64, 128), jnp.bfloat16)
    block = pl.BlockSpec((step, ROWS, HEAD_DIM), lambda i: (i, 0, 0))
    specs = ([block, block], pl.BlockSpec((step, 2, 64, 128), lambda i: (i, 0, 0, 0)))
    packed = call(
        pack_kernel, (keys, values), out, "pack", (pltpu.VMEM((step, 64, 128), jnp.float32),),
        moved=1_000_000, grid=(frames // step,), specs=specs,
    )
    return packed.reshape(2 * frames, 64, 128)


def qkv_kernel(toks, w, gain, out):
    rows = toks.shape[1]
    for i in range(toks.shape[0]):
        raw = dot(toks[i], w[...], NT)
        at = slice(i * rows, (i + 1) * rows)
        out[0, at] = head_norm(raw[:, :HEAD_DIM], gain[0:1])
        out[1, at] = head_norm(raw[:, HEAD_DIM : 2 * HEAD_DIM], gain[1:2])
        out[2, at] = raw[:, 2 * HEAD_DIM :].astype(jnp.bfloat16)


def qkv(toks, w, gain):
    rows = toks.shape[0] * toks.shape[1]
    shape = jax.ShapeDtypeStruct((3, rows, HEAD_DIM), jnp.bfloat16)
    flops = 2 * rows * w.shape[0] * w.shape[1]
    return call(qkv_kernel, (toks, w, gain), shape, "qkv", flops=flops, moved=3_000_000)


def spatial_kernel(q, old, rowp, colp, out, vals_s, old_s, attn_s):
    step = pl.program_id(0)
    factor = HEAD_DIM ** (-0.5)

    @pl.when(step == 0)
    def _():
        raw = old[...].astype(jnp.float32)
        vals_s[:, :, :56] = raw[:, :56, HEAD_DIM:]
        for j in range(7):
            vals_s[:, 8 * j : 8 * j + 8, 56:72] = raw[:, 56:, 16 * j : 16 * j + 16]
        old_s[...] = raw[:, :56, :HEAD_DIM].reshape(old_s.shape).astype(jnp.bfloat16)

    at = pl.ds(pl.multiple_of(step * QBLOCK, QBLOCK), QBLOCK)
    query, key, value = q[0, at], q[1, at], q[2, at]
    old_values = vals_s[...].reshape(old_s.shape).astype(jnp.bfloat16)
    far = dot(query, old_s[...], NT)
    far = jnp.where(rowp[at] == colp[...], NEG, far)
    near = dot(query, key, NT)
    r_id = lax.broadcasted_iota(jnp.int32, (QBLOCK, QBLOCK), 0) // ROWS
    c_id = lax.broadcasted_iota(jnp.int32, (QBLOCK, QBLOCK), 1) // ROWS
    near = jnp.where(r_id == c_id, near, NEG)
    top = jnp.maximum(jnp.max(far, axis=1, keepdims=True), jnp.max(near, axis=1, keepdims=True))
    e_far = jnp.exp((far - top) * factor)
    e_near = jnp.exp((near - top) * factor)
    total = jnp.sum(e_far, axis=1, keepdims=True) + jnp.sum(e_near, axis=1, keepdims=True)
    mixed = dot(e_far.astype(jnp.bfloat16), old_values) + dot(e_near.astype(jnp.bfloat16), value)
    attn_s[...] = mixed / total
    for j in range(4):
        out[j, step] = attn_s[j * ROWS : (j + 1) * ROWS].astype(jnp.bfloat16)


def spatial(q, old, rowp, colp):
    rows = q.shape[1]
    whole = lambda a: pl.BlockSpec(a.shape, lambda i: (0,) * len(a.shape))
    out = jax.ShapeDtypeStruct((4, 4, ROWS, HEAD_DIM), jnp.bfloat16)
    args = (q, old, rowp, colp)
    specs = (
        [whole(a) for a in args],
        whole(out),
    )
    scratch = (
        pltpu.VMEM((2 * PLANE, ROWS, HEAD_DIM), jnp.float32),
        pltpu.VMEM((2 * PLANE * ROWS, HEAD_DIM), jnp.bfloat16),
        pltpu.VMEM((QBLOCK, HEAD_DIM), jnp.float32),
    )
    return call(
        spatial_kernel, args, out, "spatial", scratch, flops=600_000_000, moved=2_000_000,
        trans=1_800_000, grid=(rows // QBLOCK,), specs=specs,
    )


def heads_out_kernel(place, attn, w0, w1, w2, w3, out):
    total = sum(dot(attn[place[k]], w[...]) for k, w in enumerate((w0, w1, w2, w3)))
    for i in range(4):
        out[i] = total[i * ROWS : (i + 1) * ROWS].astype(jnp.bfloat16)


def heads_out(place, attn, ws):
    out = jax.ShapeDtypeStruct((4, ROWS, ws[0].shape[1]), jnp.bfloat16)
    vmem = pl.BlockSpec(memory_space=pltpu.VMEM)
    specs = ([pl.BlockSpec(memory_space=pltpu.SMEM)] + [vmem] * 5, vmem)
    return call(
        heads_out_kernel, (place, attn, *ws), out, "heads_out", flops=150_000_000, moved=1_200_000,
        grid=(), specs=specs,
    )


def combine_kernel(part, resid, mod, middle, hmod):
    summed = part[0].astype(jnp.float32)
    for i in range(1, part.shape[0]):
        summed = summed + part[i].astype(jnp.float32)
    mid = (resid[...].astype(jnp.float32) + mod[0:1] * summed).astype(jnp.bfloat16)
    middle[...] = mid
    hmod[...] = normed(mid.astype(jnp.float32), mod[1:2], mod[2:3])


def combine(part, resid, mod):
    out = jax.ShapeDtypeStruct(resid.shape, jnp.bfloat16)
    return call(combine_kernel, (part, resid, mod), (out, out), "combine", moved=2_500_000)


def project_kernel(heads, attn, w, resid, gate, out, attn_s, w_s, sems):
    part = w.shape[0] // 3
    pieces = [pl.ds(i * part, part) for i in range(3)]
    copies = [pltpu.make_async_copy(w.at[at], w_s.at[at], sems.at[i]) for i, at in enumerate(pieces)]
    for copy in copies:
        copy.start()
    for g in range(PLANE):
        piece = attn[heads[g]].astype(jnp.float32)
        at = g * HEAD_DIM
        attn_s[:32, at : at + 72] = piece[:, :72]
        attn_s[32:, at : at + 56] = piece[:24, 72:]
        for j in range(3):
            attn_s[32 + 8 * j : 40 + 8 * j, at + 56 : at + 72] = piece[24:, 72 + 16 * j : 88 + 16 * j]
    summed = jnp.zeros(out.shape, jnp.float32)
    for copy, at in zip(copies, pieces):
        copy.wait()
        summed = summed + dot(attn_s[:, at].astype(jnp.bfloat16), w_s[at])
    out[...] = (resid[...].astype(jnp.float32) + gate[...] * summed).astype(jnp.bfloat16)


def project(heads, attn, w, resid, gate):
    out = jax.ShapeDtypeStruct(resid.shape, jnp.bfloat16)
    vmem = pl.BlockSpec(memory_space=pltpu.VMEM)
    specs = (
        [pl.BlockSpec(memory_space=pltpu.SMEM), vmem, pl.BlockSpec(memory_space=pl.ANY), vmem, vmem],
        vmem,
    )
    scratch = (
        pltpu.VMEM(resid.shape, jnp.float32),
        pltpu.VMEM(w.shape, w.dtype),
        pltpu.SemaphoreType.DMA((3,)),
    )
    return call(
        project_kernel, (heads, attn, w, resid, gate), out, "project", scratch, flops=150_000_000,
        moved=3_200_000, grid=(), specs=specs, limit=VMEM_ALL,
    )


def temporal_kernel(place, own, other, out, packed):
    factor = HEAD_DIM ** (-0.5)
    half = own.shape[1]
    size = 2 * half * 8
    r_id = lax.broadcasted_iota(jnp.int32, (size, size), 0) % 8
    c_id = lax.broadcasted_iota(jnp.int32, (size, size), 1) % 8
    same = r_id == c_id

    for g in range(ROWS // 8):
        at = slice(8 * g, 8 * g + 8)

        def pick(i):
            return jnp.concatenate(
                [r[i, f, at].astype(jnp.float32) for r in (own, other) for f in range(half)], axis=0
            ).astype(jnp.bfloat16)

        scores = jnp.where(same, dot(pick(0), pick(1), NT), NEG)
        top = jnp.max(scores, axis=1, keepdims=True)
        expo = jnp.exp((scores - top) * factor)
        weights = (expo / jnp.sum(expo, axis=1, keepdims=True)).astype(jnp.bfloat16)
        mixed = dot(weights, pick(2)).reshape(2 * half, 8, HEAD_DIM)
        if g < 4:
            packed[:, at, :72] = mixed
        else:
            packed[:, slice(8 * g - 32, 8 * g - 24), 72:] = mixed[:, :, :56]
            packed[:, 24:, 72 + 16 * (g - 4) : 88 + 16 * (g - 4)] = mixed[:, :, 56:]

    packed[:, 24:, 120:] = jnp.zeros_like(packed[:, 24:, 120:])
    for f in range(2 * half):
        out[place[f]] = packed[f].astype(jnp.bfloat16)


def temporal(place, own, other):
    frames = 2 * own.shape[1]
    shape = jax.ShapeDtypeStruct((frames, 32, 128), jnp.bfloat16)
    vmem = pl.BlockSpec(memory_space=pltpu.VMEM)
    specs = ([pl.BlockSpec(memory_space=pltpu.SMEM), vmem, vmem], vmem)
    return call(
        temporal_kernel, (place, own, other), shape, "temporal", (pltpu.VMEM((frames, 32, 128), jnp.float32),),
        flops=50_000_000, moved=1_000_000, trans=120_000, grid=(), specs=specs,
    )


def flat(z, c, x, y, h):
    index = 0
    for value, size in zip((z, c, x, y, h), SIZES):
        index = index * size + value
    return index


def turn(z):
    return 2 * z + 8 * (z % 2)


def shifted():
    pairs = []
    for x in range(4):
        for y in range(4):
            q = 4 * x + y
            for ring in range(16):
                step = (((q + turn(ring % 8)) % 16) // 2 - ring % 8) % 8
                if step > 4 or (step == 4 and ring // 2 % 2):
                    step -= 8
                a, b = (ring + step) % 16, ring
                pairs.append((flat(a % 8, q % 2, x, y, a // 8), flat(b % 8, q % 2, x, y, b // 8)))
    return pairs


def rolled():
    return [
        [flat(z, c, q // 4, q % 4, h) for q in ((i - turn(z)) % PLANE for i in range(PLANE))]
        for z in range(8)
        for c in range(2)
        for h in range(2)
    ]


SWAP = [(0, 1), (1, 0)]


def xor_gather(blocks, axis):
    send = lambda k: lax.ppermute(blocks[k], axis, [(i, i ^ k) for i in range(4)])
    return [blocks[0]] + [send(k) for k in (1, 2, 3)]


LOOP = (0, 2, 4, 6, 7, 5, 3, 1)


def line_gather(block):
    return lax.all_gather(block, "z", axis=0, axis_index_groups=[list(LOOP)])


def local(stream, stale_keys, stale_values, modulation, w_qkv, w_out, qk_gain):
    width = stream.shape[2]
    x, y, z, c, h = [lax.axis_index(a) for a in ("x", "y", "z", "c", "h")]
    mine = y % 2 == c
    blocks = jnp.arange(16, dtype=jnp.int32)

    hmod = modulate(stream[0], modulation[0])
    toks = lax.all_gather(hmod, ("x", "y"), axis=0).reshape(4, QBLOCK, width)

    chunk = pack(stale_keys, stale_values)
    old = lax.all_to_all(chunk, ("z", "c", "h"), 0, 0, tiled=True)

    rows = jnp.concatenate([w_qkv[0].reshape(3 * HEAD_DIM, width), w_out[0], w_out[1]], axis=0)
    rows = lax.ppermute(rows, AXES, shifted())
    rows = jnp.where(mine, rows, lax.ppermute(rows, "c", SWAP))
    w_col, w_head, w_last = (
        rows[: 3 * HEAD_DIM], rows[3 * HEAD_DIM : 4 * HEAD_DIM], rows[4 * HEAD_DIM :]
    )
    old = lax.all_to_all(
        old.reshape(16, 2, 64, 128), AXES, 0, 0, axis_index_groups=rolled(), tiled=True
    )

    toks, late = lax.optimization_barrier((toks, w_head))
    w_heads = xor_gather((w_head, w_head, w_head, late), "y")
    fresh = qkv(toks, w_col, qk_gain[0])
    rowp = jnp.repeat(2 * blocks + h, ROWS)[:, None]
    colp = jnp.repeat((lax.iota(jnp.int32, 2 * PLANE) - 2 * turn(z)) % (2 * PLANE), ROWS)[None, :]
    attn = spatial(fresh, old.reshape(2 * PLANE, 64, 128), rowp, colp)
    attn, w_heads = lax.optimization_barrier((attn, w_heads))
    attn = lax.all_to_all(attn, "y", 0, 0, tiled=True)
    attn, w_last, w_own = lax.optimization_barrier(
        (attn, w_last, w_qkv[1].reshape(3 * HEAD_DIM, width))
    )
    w_last = lax.all_gather(w_last, ("x", "y"), axis=0).reshape(width, width)
    part = heads_out(y ^ blocks[:4], attn.reshape(4, QBLOCK, HEAD_DIM), w_heads)
    part = lax.all_to_all(part, "x", 0, 0, tiled=True)
    middle, hmod = combine(part, stream[0], jnp.concatenate([modulation[0, 2:], modulation[1, :2]]))

    toks = line_gather(hmod).reshape(1, 8 * ROWS, width)
    w_sib = lax.ppermute(w_own, "c", SWAP)
    sib = qkv(toks, w_sib, qk_gain[1])
    other = lax.ppermute(sib, "c", SWAP)
    own = qkv(toks, w_own, qk_gain[1])
    shape = (3, 8, ROWS, HEAD_DIM)
    place = 2 * jnp.array(LOOP * 2, jnp.int32) + (c ^ (blocks // 8))
    attn = temporal(place, own.reshape(shape), other.reshape(shape))
    attn = lax.all_to_all(attn, ("z", "c"), 0, 0, tiled=True)
    out = project((blocks + turn(z)) % 16, attn, w_last, middle, modulation[1, 2:])
    return out[None]


def solution(mesh):
    wide = Mesh(mesh.devices.reshape(SIZES), AXES)
    tm, patch = ("z", "c"), ("x", "y", "h")
    placed = (
        P(tm, patch, None),
        P(None, patch, tm),
        P(None, patch, tm),
        P(),
        P(None, None, tm, None),
        P(None, tm, None),
        P(),
    )
    return jax.shard_map(
        local, mesh=wide, in_specs=placed, out_specs=P(tm, patch, None), check_vma=False
    )
```

```python
import math

import jax
import jax.numpy as jnp
from jax import lax
from jax.experimental import pallas as pl
from jax.experimental.pallas import tpu as pltpu
from jax.sharding import Mesh
from jax.sharding import PartitionSpec as P

HEAD_DIM = 72
EPS = 1e-06
AXES = ("z", "c", "x", "y", "h")
SIZES = (8, 2, 4, 4, 2)
ROWS = 56
PLANE = 16
QBLOCK = 4 * ROWS
NEG = -1e30
VMEM_LIMIT = 20 * 1024 * 1024
VMEM_ALL = 60 * 1024 * 1024
NT = (((1,), (1,)), ((), ()))


def normed(values, shift, scale):
    center = jnp.mean(values, axis=-1, keepdims=True)
    spread = jnp.mean(jnp.square(values - center), axis=-1, keepdims=True)
    unit = (values - center) * lax.rsqrt(spread + EPS)
    return (unit * (1.0 + scale) + shift).astype(jnp.bfloat16)


def head_norm(values, gain):
    factor = lax.rsqrt(jnp.mean(values * values, axis=-1, keepdims=True) + EPS)
    return (values * factor * gain).astype(jnp.bfloat16)


def dot(a, b, dims=(((1,), (0,)), ((), ()))):
    return lax.dot_general(a, b, dims, preferred_element_type=jnp.float32)


def call(
    kernel, args, out_shape, name, scratch=(), flops=0, moved=0, trans=0, grid=None, specs=None, limit=VMEM_LIMIT
):
    extra = {} if grid is None else {"grid": grid, "in_specs": specs[0], "out_specs": specs[1]}
    return pl.pallas_call(
        kernel,
        out_shape=out_shape,
        scratch_shapes=list(scratch),
        compiler_params=pltpu.CompilerParams(vmem_limit_bytes=limit),
        cost_estimate=pl.CostEstimate(flops=flops, bytes_accessed=moved, transcendentals=trans),
        name=name,
        **extra,
    )(*args)


def modulate_kernel(x, mod, out):
    out[...] = normed(x[...].astype(jnp.float32), mod[0:1], mod[1:2])


def modulate(x, mod):
    shape = jax.ShapeDtypeStruct(x.shape, jnp.bfloat16)
    return call(modulate_kernel, (x, mod), shape, "modulate", moved=300_000)


def pack_kernel(keys, values, out, scratch):
    old = values[...].astype(jnp.float32)
    scratch[:, :ROWS, :HEAD_DIM] = keys[...].astype(jnp.float32)
    scratch[:, :ROWS, HEAD_DIM:] = old[:, :, :56]
    scratch[:, ROWS:] = jnp.zeros_like(scratch[:, ROWS:])
    for j in range(7):
        scratch[:, ROWS:, 16 * j : 16 * j + 16] = old[:, 8 * j : 8 * j + 8, 56:]
    chunk = scratch[...].astype(jnp.bfloat16)
    for i in range(2):
        out[:, i] = chunk


def pack(keys, values):
    frames, step = keys.shape[0], 4
    out = jax.ShapeDtypeStruct((frames, 2, 64, 128), jnp.bfloat16)
    block = pl.BlockSpec((step, ROWS, HEAD_DIM), lambda i: (i, 0, 0))
    specs = ([block, block], pl.BlockSpec((step, 2, 64, 128), lambda i: (i, 0, 0, 0)))
    packed = call(
        pack_kernel, (keys, values), out, "pack", (pltpu.VMEM((step, 64, 128), jnp.float32),),
        moved=1_000_000, grid=(frames // step,), specs=specs,
    )
    return packed.reshape(2 * frames, 64, 128)


def qkv_kernel(toks, w, gain, out):
    rows = toks.shape[1]
    for i in range(toks.shape[0]):
        raw = dot(toks[i], w[...], NT)
        at = slice(i * rows, (i + 1) * rows)
        out[0, at] = head_norm(raw[:, :HEAD_DIM], gain[0:1])
        out[1, at] = head_norm(raw[:, HEAD_DIM : 2 * HEAD_DIM], gain[1:2])
        out[2, at] = raw[:, 2 * HEAD_DIM :].astype(jnp.bfloat16)


def qkv(toks, w, gain):
    rows = toks.shape[0] * toks.shape[1]
    shape = jax.ShapeDtypeStruct((3, rows, HEAD_DIM), jnp.bfloat16)
    flops = 2 * rows * w.shape[0] * w.shape[1]
    return call(qkv_kernel, (toks, w, gain), shape, "qkv", flops=flops, moved=3_000_000)


def spatial_kernel(q, old, rowp, colp, out, vals_s, old_s, val_s, attn_s):
    step = pl.program_id(0)
    factor = HEAD_DIM ** (-0.5) * math.log2(math.e)

    @pl.when(step == 0)
    def _():
        raw = old[...].astype(jnp.float32)
        vals_s[:, :, :56] = raw[:, :56, HEAD_DIM:]
        for j in range(7):
            vals_s[:, 8 * j : 8 * j + 8, 56:72] = raw[:, 56:, 16 * j : 16 * j + 16]
        old_s[...] = raw[:, :56, :HEAD_DIM].reshape(old_s.shape).astype(jnp.bfloat16)
        val_s[...] = vals_s[...].reshape(old_s.shape).astype(jnp.bfloat16)

    at = pl.ds(pl.multiple_of(step * QBLOCK, QBLOCK), QBLOCK)
    query, key, value = q[0, at], q[1, at], q[2, at]
    far = dot(query, old_s[...], NT)
    far = jnp.where(rowp[at] == colp[...], NEG, far)
    near = dot(query, key, NT)
    r_id = lax.broadcasted_iota(jnp.int32, (QBLOCK, QBLOCK), 0) // ROWS
    c_id = lax.broadcasted_iota(jnp.int32, (QBLOCK, QBLOCK), 1) // ROWS
    near = jnp.where(r_id == c_id, near, NEG)
    top = jnp.maximum(jnp.max(far, axis=1, keepdims=True), jnp.max(near, axis=1, keepdims=True))
    e_far = jnp.exp2((far - top) * factor)
    e_near = jnp.exp2((near - top) * factor)
    total = jnp.sum(e_far, axis=1, keepdims=True) + jnp.sum(e_near, axis=1, keepdims=True)
    mixed = dot(e_far.astype(jnp.bfloat16), val_s[...]) + dot(e_near.astype(jnp.bfloat16), value)
    attn_s[...] = mixed / total
    for j in range(4):
        out[j, step] = attn_s[j * ROWS : (j + 1) * ROWS].astype(jnp.bfloat16)


def spatial(q, old, rowp, colp):
    rows = q.shape[1]
    whole = lambda a: pl.BlockSpec(a.shape, lambda i: (0,) * len(a.shape))
    out = jax.ShapeDtypeStruct((4, 4, ROWS, HEAD_DIM), jnp.bfloat16)
    args = (q, old, rowp, colp)
    specs = (
        [whole(a) for a in args],
        whole(out),
    )
    scratch = (
        pltpu.VMEM((2 * PLANE, ROWS, HEAD_DIM), jnp.float32),
        pltpu.VMEM((2 * PLANE * ROWS, HEAD_DIM), jnp.bfloat16),
        pltpu.VMEM((2 * PLANE * ROWS, HEAD_DIM), jnp.bfloat16),
        pltpu.VMEM((QBLOCK, HEAD_DIM), jnp.float32),
    )
    return call(
        spatial_kernel, args, out, "spatial", scratch, flops=600_000_000, moved=2_000_000,
        trans=1_800_000, grid=(rows // QBLOCK,), specs=specs,
    )


def heads_out_kernel(place, attn, w0, w1, w2, w3, out):
    total = sum(dot(attn[place[k]], w[...]) for k, w in enumerate((w0, w1, w2, w3)))
    for i in range(4):
        out[i] = total[i * ROWS : (i + 1) * ROWS].astype(jnp.bfloat16)


def heads_out(place, attn, ws):
    out = jax.ShapeDtypeStruct((4, ROWS, ws[0].shape[1]), jnp.bfloat16)
    vmem = pl.BlockSpec(memory_space=pltpu.VMEM)
    specs = ([pl.BlockSpec(memory_space=pltpu.SMEM)] + [vmem] * 5, vmem)
    return call(
        heads_out_kernel, (place, attn, *ws), out, "heads_out", flops=150_000_000, moved=1_200_000,
        grid=(), specs=specs,
    )


def combine_kernel(part, resid, mod, middle, hmod):
    summed = part[0].astype(jnp.float32)
    for i in range(1, part.shape[0]):
        summed = summed + part[i].astype(jnp.float32)
    mid = (resid[...].astype(jnp.float32) + mod[0:1] * summed).astype(jnp.bfloat16)
    middle[...] = mid
    hmod[...] = normed(mid.astype(jnp.float32), mod[1:2], mod[2:3])


def combine(part, resid, mod):
    out = jax.ShapeDtypeStruct(resid.shape, jnp.bfloat16)
    return call(combine_kernel, (part, resid, mod), (out, out), "combine", moved=2_500_000)


def project_kernel(heads, attn, w, resid, gate, out, attn_s, w_s, sems):
    part = w.shape[0] // 3
    pieces = [pl.ds(i * part, part) for i in range(3)]
    copies = [pltpu.make_async_copy(w.at[at], w_s.at[at], sems.at[i]) for i, at in enumerate(pieces)]
    for copy in copies:
        copy.start()
    for g in range(PLANE):
        piece = attn[heads[g]].astype(jnp.float32)
        at = g * HEAD_DIM
        attn_s[:32, at : at + 72] = piece[:, :72]
        attn_s[32:, at : at + 56] = piece[:24, 72:]
        for j in range(3):
            attn_s[32 + 8 * j : 40 + 8 * j, at + 56 : at + 72] = piece[24:, 72 + 16 * j : 88 + 16 * j]
    summed = jnp.zeros(out.shape, jnp.float32)
    for copy, at in zip(copies, pieces):
        copy.wait()
        summed = summed + dot(attn_s[:, at].astype(jnp.bfloat16), w_s[at])
    out[...] = (resid[...].astype(jnp.float32) + gate[...] * summed).astype(jnp.bfloat16)


def project(heads, attn, w, resid, gate):
    out = jax.ShapeDtypeStruct(resid.shape, jnp.bfloat16)
    vmem = pl.BlockSpec(memory_space=pltpu.VMEM)
    specs = (
        [pl.BlockSpec(memory_space=pltpu.SMEM), vmem, pl.BlockSpec(memory_space=pl.ANY), vmem, vmem],
        vmem,
    )
    scratch = (
        pltpu.VMEM(resid.shape, jnp.float32),
        pltpu.VMEM(w.shape, w.dtype),
        pltpu.SemaphoreType.DMA((3,)),
    )
    return call(
        project_kernel, (heads, attn, w, resid, gate), out, "project", scratch, flops=150_000_000,
        moved=3_200_000, grid=(), specs=specs, limit=VMEM_ALL,
    )


def temporal_kernel(place, own, other, out, packed):
    factor = HEAD_DIM ** (-0.5)
    half = own.shape[1]
    size = 2 * half * 8
    r_id = lax.broadcasted_iota(jnp.int32, (size, size), 0) % 8
    c_id = lax.broadcasted_iota(jnp.int32, (size, size), 1) % 8
    same = r_id == c_id

    for g in range(ROWS // 8):
        at = slice(8 * g, 8 * g + 8)

        def pick(i):
            return jnp.concatenate(
                [r[i, f, at].astype(jnp.float32) for r in (own, other) for f in range(half)], axis=0
            ).astype(jnp.bfloat16)

        scores = jnp.where(same, dot(pick(0), pick(1), NT), NEG)
        top = jnp.max(scores, axis=1, keepdims=True)
        expo = jnp.exp((scores - top) * factor)
        weights = (expo / jnp.sum(expo, axis=1, keepdims=True)).astype(jnp.bfloat16)
        mixed = dot(weights, pick(2)).reshape(2 * half, 8, HEAD_DIM)
        if g < 4:
            packed[:, at, :72] = mixed
        else:
            packed[:, slice(8 * g - 32, 8 * g - 24), 72:] = mixed[:, :, :56]
            packed[:, 24:, 72 + 16 * (g - 4) : 88 + 16 * (g - 4)] = mixed[:, :, 56:]

    packed[:, 24:, 120:] = jnp.zeros_like(packed[:, 24:, 120:])
    for f in range(2 * half):
        out[place[f]] = packed[f].astype(jnp.bfloat16)


def temporal(place, own, other):
    frames = 2 * own.shape[1]
    shape = jax.ShapeDtypeStruct((frames, 32, 128), jnp.bfloat16)
    vmem = pl.BlockSpec(memory_space=pltpu.VMEM)
    specs = ([pl.BlockSpec(memory_space=pltpu.SMEM), vmem, vmem], vmem)
    return call(
        temporal_kernel, (place, own, other), shape, "temporal", (pltpu.VMEM((frames, 32, 128), jnp.float32),),
        flops=50_000_000, moved=1_000_000, trans=120_000, grid=(), specs=specs,
    )


def flat(z, c, x, y, h):
    index = 0
    for value, size in zip((z, c, x, y, h), SIZES):
        index = index * size + value
    return index


def turn(z):
    return 2 * z + 8 * (z % 2)


def shifted():
    pairs = []
    for x in range(4):
        for y in range(4):
            q = 4 * x + y
            for ring in range(16):
                step = (((q + turn(ring % 8)) % 16) // 2 - ring % 8) % 8
                if step > 4 or (step == 4 and ring // 2 % 2):
                    step -= 8
                a, b = (ring + step) % 16, ring
                pairs.append((flat(a % 8, q % 2, x, y, a // 8), flat(b % 8, q % 2, x, y, b // 8)))
    return pairs


def rolled():
    return [
        [flat(z, c, q // 4, q % 4, h) for q in ((i - turn(z)) % PLANE for i in range(PLANE))]
        for z in range(8)
        for c in range(2)
        for h in range(2)
    ]


SWAP = [(0, 1), (1, 0)]


def xor_gather(blocks, axis):
    send = lambda k: lax.ppermute(blocks[k], axis, [(i, i ^ k) for i in range(4)])
    return [blocks[0]] + [send(k) for k in (1, 2, 3)]


LOOP = (0, 2, 4, 6, 7, 5, 3, 1)


def line_gather(block):
    return lax.all_gather(block, "z", axis=0, axis_index_groups=[list(LOOP)])


def local(stream, stale_keys, stale_values, modulation, w_qkv, w_out, qk_gain):
    width = stream.shape[2]
    x, y, z, c, h = [lax.axis_index(a) for a in ("x", "y", "z", "c", "h")]
    mine = y % 2 == c
    blocks = jnp.arange(16, dtype=jnp.int32)

    hmod = modulate(stream[0], modulation[0])
    toks = lax.all_gather(hmod, ("x", "y"), axis=0).reshape(4, QBLOCK, width)

    chunk = pack(stale_keys, stale_values)
    old = lax.all_to_all(chunk, ("z", "c", "h"), 0, 0, tiled=True)

    rows = jnp.concatenate([w_qkv[0].reshape(3 * HEAD_DIM, width), w_out[0], w_out[1]], axis=0)
    rows = lax.ppermute(rows, AXES, shifted())
    rows = jnp.where(mine, rows, lax.ppermute(rows, "c", SWAP))
    w_col, w_head, w_last = (
        rows[: 3 * HEAD_DIM], rows[3 * HEAD_DIM : 4 * HEAD_DIM], rows[4 * HEAD_DIM :]
    )
    old = lax.all_to_all(
        old.reshape(16, 2, 64, 128), AXES, 0, 0, axis_index_groups=rolled(), tiled=True
    )

    toks, late = lax.optimization_barrier((toks, w_head))
    w_heads = xor_gather((w_head, w_head, w_head, late), "y")
    fresh = qkv(toks, w_col, qk_gain[0])
    rowp = jnp.repeat(2 * blocks + h, ROWS)[:, None]
    colp = jnp.repeat((lax.iota(jnp.int32, 2 * PLANE) - 2 * turn(z)) % (2 * PLANE), ROWS)[None, :]
    attn = spatial(fresh, old.reshape(2 * PLANE, 64, 128), rowp, colp)
    attn, w_heads = lax.optimization_barrier((attn, w_heads))
    attn = lax.all_to_all(attn, "y", 0, 0, tiled=True)
    attn, w_last, w_own = lax.optimization_barrier(
        (attn, w_last, w_qkv[1].reshape(3 * HEAD_DIM, width))
    )
    w_last = lax.all_gather(w_last, ("x", "y"), axis=0).reshape(width, width)
    part = heads_out(y ^ blocks[:4], attn.reshape(4, QBLOCK, HEAD_DIM), w_heads)
    part = lax.all_to_all(part, "x", 0, 0, tiled=True)
    middle, hmod = combine(part, stream[0], jnp.concatenate([modulation[0, 2:], modulation[1, :2]]))

    toks = line_gather(hmod).reshape(1, 8 * ROWS, width)
    w_sib = lax.ppermute(w_own, "c", SWAP)
    sib = qkv(toks, w_sib, qk_gain[1])
    other = lax.ppermute(sib, "c", SWAP)
    own = qkv(toks, w_own, qk_gain[1])
    shape = (3, 8, ROWS, HEAD_DIM)
    place = 2 * jnp.array(LOOP * 2, jnp.int32) + (c ^ (blocks // 8))
    attn = temporal(place, own.reshape(shape), other.reshape(shape))
    attn = lax.all_to_all(attn, ("z", "c"), 0, 0, tiled=True)
    out = project((blocks + turn(z)) % 16, attn, w_last, middle, modulation[1, 2:])
    return out[None]


def solution(mesh):
    wide = Mesh(mesh.devices.reshape(SIZES), AXES)
    tm, patch = ("z", "c"), ("x", "y", "h")
    placed = (
        P(tm, patch, None),
        P(None, patch, tm),
        P(None, patch, tm),
        P(),
        P(None, None, tm, None),
        P(None, tm, None),
        P(),
    )
    return jax.shard_map(
        local, mesh=wide, in_specs=placed, out_specs=P(tm, patch, None), check_vma=False
    )
```
